512 devices in a mesh: seg: 16 (over z, core), chan: 32 (over y, x).
Axes of the slice: x: 4, y: 8, z: 8, core: 2. Of those that a mesh axis runs over, the one named last changes fastest.
Arguments:
- das_records: float32 [16384, 8, 1500], P(('seg', 'chan')), may hold values from -6 to 6
- source_ids: int32 [4, 2], replicated, may hold values from 0 to 16383
- near_pairs: int32 [65536, 2], P(('seg', 'chan')), may hold values from 0 to 16383, as said below
- pair_count: int32 [512], P(('seg', 'chan')), may hold values from 64 to 128, as said below
Outputs:
- source_xcorr: float32 [4, 2, 16384, 256], P(None, None, ('seg', 'chan'))
- pair_xcorr: float32 [65536, 256], P(('seg', 'chan'))
The draws below stay inside these ranges and needn't reach their ends.
Inputs may be any that keep to these rules, and one draw needn't show every extreme that they name: `near_pairs`: every slot, live or not, holds valid channels: the first lies in the block of 32 channels of the slot's device, the second 1 to 8 channels away from it; the offset 8 occurs on every device. `pair_count`: some device has all 128 slots live.
All inputs are finite; a program needn't handle non-finite values.
Results may differ from the reference program's by a relative error of at most 0.0003.
Values sent between devices are 32-bit elements; how exact they have to be, the bound alone decides.
A program may use at most 64 MiB of HBM per device.

```python
import math
import jax
import jax.numpy as jnp
from jax import lax

CH_DEV = 32
WIN = 8
L = 1500
FLO = 30
NB = 512
SMOOTH = 4
LAGS = 256
ROUNDS = 4
MAXOFF = 8
PMAX = 128
CHANNELS = 16384
NPAIRS = 65536


def draw_pair_count(key, part):
    groups = NPAIRS // PMAX
    count_key = jax.random.fold_in(key, 11)
    pick_key = jax.random.fold_in(key, 13)
    counts = jax.random.randint(count_key, (groups,), PMAX // 2, PMAX + 1)
    chosen = jax.random.randint(pick_key, (), 0, groups)
    return counts.at[chosen].set(PMAX).astype(jnp.int32)


def draw_near_pairs(key, part):
    slot_device = jnp.arange(NPAIRS, dtype=jnp.int32) // PMAX
    within = jax.random.randint(jax.random.fold_in(key, 21), (NPAIRS,), 0, CH_DEV)
    steps = jax.random.randint(jax.random.fold_in(key, 22), (NPAIRS,), 1, MAXOFF + 1)
    steps = steps.at[::PMAX].set(MAXOFF)
    signs = 2 * jax.random.randint(jax.random.fold_in(key, 23), (NPAIRS,), 0, 2) - 1
    first_chan = slot_device * CH_DEV + within
    second_chan = first_chan + signs * steps
    outside = (second_chan < 0) | (second_chan >= CHANNELS)
    second_chan = jnp.where(outside, first_chan - signs * steps, second_chan)
    return jnp.stack([first_chan, second_chan], axis=1).astype(jnp.int32)


def with_ends(drawn, key, least, high):
    spot = [jax.random.randint(jax.random.fold_in(key, axis), (), 0, length) for axis, length in enumerate(drawn.shape)]
    longest = drawn.shape.index(max(drawn.shape))
    next_to = spot[:longest] + [(spot[longest] + 1) % drawn.shape[longest]] + spot[longest + 1:]
    return drawn.at[tuple(spot)].set(least).at[tuple(next_to)].set(high)


def block_scale(key, dims, cuts, low, high):
    loudness = 1.0
    for axis_at, blocks in cuts:
        steps = jax.random.uniform(jax.random.fold_in(jax.random.fold_in(key, 6), axis_at), (blocks,), jnp.float32, low / len(cuts), high / len(cuts))
        loudness = loudness * jnp.repeat(jnp.exp(steps), dims[axis_at] // blocks).reshape((-1,) + (1,) * (len(dims) - 1 - axis_at))
    return loudness


def normal_values(rng, shape, spread, bound, shards=(), kind=jnp.bfloat16):
    values = jax.random.normal(rng, shape, jnp.float32) * spread
    if len(shards) > 0:
        values = block_scale(rng, shape, shards, -0.22, 0.18) * values
    return jnp.clip(values, min=-bound, max=bound).astype(kind)


def setup_inputs(seed: int = 0) -> dict:
    keys = jax.random.split(jax.random.key(seed), 5)
    das_records = normal_values(keys[0], (CHANNELS, WIN, L), 1.0, 6.0, ((0, 512),), jnp.float32)
    source_ids = with_ends(jax.random.randint(keys[1], (ROUNDS, 2), 0, CHANNELS), jax.random.fold_in(keys[1], 1), 0, CHANNELS - 1).astype(jnp.int32)
    near_pairs = draw_near_pairs(jax.random.fold_in(keys[4], 71), 0)
    pair_count = draw_pair_count(jax.random.fold_in(keys[4], 71), 0)
    return dict(das_records=das_records, source_ids=source_ids, near_pairs=near_pairs, pair_count=pair_count)


clip_level = 2.0
water_level = 0.1
epsilon = 1e-06

def normalize(records):
    centered = records - lax.optimization_barrier(jnp.mean(records, axis=-1, keepdims=True))
    root_mean = jnp.sqrt(lax.optimization_barrier(jnp.mean(centered * centered, axis=-1, keepdims=True)) + epsilon)
    return jnp.clip(centered / root_mean, -clip_level, clip_level)

def whiten(spectrum):
    real_part = spectrum[..., :NB]
    imag_part = spectrum[..., NB:]
    amplitude = jnp.sqrt(real_part * real_part + imag_part * imag_part)
    widths = [(0, 0)] * (amplitude.ndim - 1) + [(SMOOTH, SMOOTH)]
    padded = jnp.pad(amplitude, widths, mode='edge')
    smoothed = padded[..., 0:NB]
    for k in range(1, 2 * SMOOTH + 1):
        smoothed = smoothed + padded[..., k:k + NB]
    denominator = smoothed / (2 * SMOOTH + 1) + water_level * lax.optimization_barrier(jnp.mean(amplitude, axis=-1, keepdims=True)) + epsilon
    return spectrum / jnp.concatenate([denominator, denominator], axis=-1)

def correlate(left_spec, right_spec):
    left_real, left_imag = (left_spec[..., :NB], left_spec[..., NB:])
    right_real, right_imag = (right_spec[..., :NB], right_spec[..., NB:])
    cross_real = lax.optimization_barrier(jnp.sum(left_real * right_real + left_imag * right_imag, axis=-2))
    cross_imag = lax.optimization_barrier(jnp.sum(left_real * right_imag - left_imag * right_real, axis=-2))
    return jnp.concatenate([cross_real, cross_imag], axis=-1)

def lag_table():
    bin_idx = FLO + jnp.arange(NB, dtype=jnp.int32)
    lag_idx = jnp.arange(LAGS, dtype=jnp.int32) - LAGS // 2
    phase_index = bin_idx[:, None] * lag_idx[None, :] % L
    phases = phase_index.astype(jnp.float32) * (2.0 * math.pi / L)
    scale = 1.0 / math.sqrt(WIN * NB)
    return jnp.concatenate([jnp.cos(phases), -jnp.sin(phases)], axis=0) * scale

def reference(das_records, source_ids, near_pairs, pair_count):
    precise = lax.Precision.HIGHEST
    blocks = das_records.reshape(CHANNELS // CH_DEV, CH_DEV, WIN, L)

    def transform(channel_block):
        normed = normalize(channel_block)
        full_spec = jnp.fft.rfft(normed, axis=-1)[..., FLO:FLO + NB]
        return whiten(jnp.concatenate([jnp.real(full_spec), jnp.imag(full_spec)], axis=-1))
    spectra = lax.map(transform, blocks).reshape(CHANNELS, WIN, 2 * NB)
    inverse = lag_table()
    sources = jnp.take(spectra, source_ids.reshape(-1), axis=0)
    count_src = sources.shape[0]

    def source_block(channel_block):
        cross_spec = correlate(sources[:, None], channel_block[None])
        flat = cross_spec.reshape(count_src * CH_DEV, 2 * NB)
        return jnp.dot(flat, inverse, precision=precise).reshape(count_src, CH_DEV, LAGS)
    per_block = lax.map(source_block, spectra.reshape(CHANNELS // CH_DEV, CH_DEV, WIN, 2 * NB))
    source_xcorr = jnp.transpose(per_block, (1, 0, 2, 3)).reshape(ROUNDS, 2, CHANNELS, LAGS)

    def pair_block(packed):
        pair_rows, count_live = packed
        left_rows = jnp.take(spectra, pair_rows[:, 0], axis=0)
        right_rows = jnp.take(spectra, pair_rows[:, 1], axis=0)
        result = jnp.dot(correlate(left_rows, right_rows), inverse, precision=precise)
        live_mask = (jnp.arange(PMAX, dtype=jnp.int32) < count_live).astype(result.dtype)
        return result * live_mask[:, None]
    groups = NPAIRS // PMAX
    pair_xcorr = lax.map(pair_block, (near_pairs.reshape(groups, PMAX, 2), pair_count)).reshape(NPAIRS, LAGS)
    return (source_xcorr, pair_xcorr)
```

```python
import functools
import math

import jax
import jax.numpy as jnp
import ml_dtypes
import numpy as np
from jax import lax
from jax.experimental import pallas as pl
from jax.experimental.pallas import tpu as pltpu
from jax.sharding import PartitionSpec as P

WIN = 8
L = 1500
HALF = L // 2
LPAD = 1536
KPAD = 768
FLO = 30
NB = 512
EVEN = NB // 2
SMOOTH = 4
LAGS = 256
SOURCES = 8
NEAR = 8
TILES = 8
LANES = 128
CORES = 2
X_CHIPS = 4

clip_level = 2.0
water_level = 0.1
epsilon = 1e-06

MESH = pl.DeviceIdType.MESH
VMEM_LIMIT = 48 * 1024 * 1024


def split(table):
    high = table.astype(np.float32).astype(ml_dtypes.bfloat16)
    low = (table - high.astype(np.float64)).astype(np.float32).astype(ml_dtypes.bfloat16)
    return high, low


def bin_order():
    return np.concatenate([np.arange(0, NB, 2), np.arange(1, NB, 2)])


@functools.lru_cache(maxsize=None)
def band_tables():
    sample = np.arange(HALF)
    out = np.zeros((2, 2, KPAD, NB), ml_dtypes.bfloat16)
    for parity in range(2):
        freq = FLO + np.arange(parity, NB, 2)
        phase = (sample[:, None] * freq[None, :] % L) * (2.0 * math.pi / L)
        table = np.concatenate([np.cos(phase), -np.sin(phase)], axis=1)
        out[parity, 0, :HALF], out[parity, 1, :HALF] = split(table)
    return out


@functools.lru_cache(maxsize=None)
def lag_tables():
    freq = FLO + bin_order()
    lag = np.arange(LAGS) - LAGS // 2
    phase = (freq[:, None] * lag[None, :] % L) * (2.0 * math.pi / L)
    table = np.concatenate([np.cos(phase), -np.sin(phase)], axis=0) / math.sqrt(WIN * NB)
    return np.stack(split(table))


@functools.lru_cache(maxsize=None)
def smooth_table():
    count = np.zeros((NB, NB))
    for centre in range(NB):
        for step in range(-SMOOTH, SMOOTH + 1):
            count[min(max(centre + step, 0), NB - 1), centre] += 1
    order = bin_order()
    return count[order][:, order].astype(ml_dtypes.bfloat16)


def dot(a, b):
    return jnp.dot(a, b, preferred_element_type=jnp.float32)


def halves(value):
    high = value.astype(jnp.bfloat16)
    return high, (value - high.astype(jnp.float32)).astype(jnp.bfloat16)


def dot3(value, high_table, low_table):
    high, low = halves(value)
    return dot(high, high_table) + dot(low, high_table) + dot(high, low_table)


def spectra_of(records, padded, band, smooth):
    centered = records - jnp.sum(records, axis=-1, keepdims=True) * (1.0 / L)
    power = jnp.sum(centered * centered, axis=-1, keepdims=True) * (1.0 / L)
    normed = jnp.clip(centered * (1.0 / jnp.sqrt(power + epsilon)), -clip_level, clip_level)
    padded[:, :L] = normed
    first = padded[:, :KPAD]
    second = pltpu.roll(padded[...], LPAD - HALF, 1)[:, :KPAD]
    even = dot3(first + second, band[0, 0], band[0, 1])
    odd = dot3(first - second, band[1, 0], band[1, 1])
    real = jnp.concatenate([even[:, :EVEN], odd[:, :EVEN]], axis=1)
    imag = jnp.concatenate([even[:, EVEN:], odd[:, EVEN:]], axis=1)
    amplitude = jnp.sqrt(real * real + imag * imag)
    high, low = halves(amplitude)
    smoothed = (dot(high, smooth[...]) + dot(low, smooth[...])) * (1.0 / (2 * SMOOTH + 1))
    mean = jnp.sum(amplitude, axis=-1, keepdims=True) * (water_level / NB)
    scale = 1.0 / (smoothed + mean + epsilon)
    return real * scale, imag * scale


def local_kernel(ids, records, band, smooth, spectra, kept, padded):
    base = (lax.axis_index("seg") * lax.axis_size("chan") + lax.axis_index("chan")) * records.shape[0]
    channels = records.shape[0]
    chunk = 16
    rows = chunk * WIN
    padded[:, LPAD - LANES :] = jnp.zeros((rows, LANES), jnp.float32)
    for start in range(0, channels, chunk):
        block = records[start : start + chunk].reshape(rows, L)
        real, imag = spectra_of(block, padded, band, smooth)
        spectra[start : start + chunk, :, :NB] = real.reshape(chunk, WIN, NB)
        spectra[start : start + chunk, :, NB:] = imag.reshape(chunk, WIN, NB)
    for s in range(SOURCES):
        local = ids[s] - base
        mine = jnp.logical_and(local >= 0, local < channels)
        row = spectra[jnp.clip(local, 0, channels - 1)]
        row = row * mine.astype(jnp.float32)
        for t in range(TILES):
            kept[s, t] = row[:, t * LANES : (t + 1) * LANES]


def exchange_kernel(dims, kept, spectra, sources, below, above, half, part, piece, r0, r1, r2, r3,
                    send, recv):
    xs, ys, zs = dims
    seg, chan = lax.axis_index("seg"), lax.axis_index("chan")
    z, core = seg // CORES, lax.rem(seg, CORES)
    y, x = chan // xs, lax.rem(chan, xs)
    per_core = SOURCES // CORES
    per_rank = per_core // xs
    per_y = TILES // ys
    channels = spectra.shape[0]
    total = lax.axis_size("seg") * lax.axis_size("chan")
    n_chan = lax.axis_size("chan")
    me = seg * n_chan + chan

    def at(z_, core_, y_, x_):
        return (z_ * CORES + core_, y_ * xs + x_)

    def of(index):
        return (index // n_chan, lax.rem(index, n_chan))

    sibling = at(z, 1 - core, y, x)
    x_peers = [(d, lax.rem(x + d, xs)) for d in range(1, xs)]
    y_peers = [(d, lax.rem(y + d, ys)) for d in range(1, ys)]
    z_peers = [(d, lax.rem(z + d, zs)) for d in range(1, zs)]
    after = of(lax.rem(me + 1, total))
    before = of(lax.rem(me + total - 1, total))

    barrier = pltpu.get_barrier_semaphore()
    greeted = [sibling, after, before]
    greeted += [at(z, core, y, p) for _, p in x_peers]
    greeted += [at(z, core, p, x) for _, p in y_peers]
    greeted += [at(p, core, y, x) for _, p in z_peers]
    for device in greeted:
        pl.semaphore_signal(barrier, inc=1, device_id=device, device_id_type=MESH)
    pl.semaphore_wait(barrier, len(greeted))

    slot = [0]

    def push(src, dst, device):
        k = slot[0]
        slot[0] += 1
        copy = pltpu.make_async_remote_copy(
            src_ref=src, dst_ref=dst, send_sem=send.at[k], recv_sem=recv.at[k],
            device_id=device, device_id_type=MESH)
        copy.start()
        return copy

    everything = []
    c0 = push(kept.at[pl.ds(per_core * (1 - core), per_core)], r0, sibling)
    up = push(spectra.at[pl.ds(channels - NEAR, NEAR)], below, after)
    down = push(spectra.at[pl.ds(0, NEAR)], above, before)
    c0.wait_recv()
    half[...] = kept[pl.ds(per_core * core, per_core)] + r0[...]
    c1 = [push(half.at[pl.ds(p * per_rank, per_rank)], r1.at[d - 1], at(z, core, y, p)) for d, p in x_peers]
    for c in c1:
        c.wait_recv()
    total_1 = half[pl.ds(x * per_rank, per_rank)]
    for d in range(xs - 1):
        total_1 += r1[d]
    part[...] = total_1
    c2 = [push(part.at[:, pl.ds(p * per_y, per_y)], r2.at[d - 1], at(z, core, p, x)) for d, p in y_peers]
    for c in c2:
        c.wait_recv()
    total_2 = part[:, pl.ds(y * per_y, per_y)]
    for d in range(ys - 1):
        total_2 += r2[d]
    piece[...] = total_2
    c3 = [push(piece, r3.at[d - 1], at(p, core, y, x)) for d, p in z_peers]
    for c in c3:
        c.wait_recv()
    for d in range(zs - 1):
        total_2 += r3[d]
    rank = (core * xs + x) * per_rank
    mine = sources.at[pl.ds(rank, per_rank), pl.ds(y * per_y, per_y)]
    mine[...] = total_2
    c4 = [push(mine, mine, at(z, core, p, x)) for d, p in y_peers]
    for c in c4:
        c.wait_recv()
    owned = sources.at[pl.ds(rank, per_rank)]
    c5 = [push(owned, owned, at(z, core, y, p)) for d, p in x_peers]
    c6 = [push(owned, owned, sibling)]
    for c, (d, _) in zip(c5, x_peers):
        c.wait_recv()
        origin = (core * xs + lax.rem(x + xs - d, xs)) * per_rank
        got = sources.at[pl.ds(origin, per_rank)]
        c6.append(push(got, got, sibling))
    for c in c6:
        c.wait_recv()
    up.wait_recv()
    down.wait_recv()
    for c in [c0, up, down] + c1 + c2 + c3 + c4 + c5 + c6:
        c.wait_send()


def result_kernel(pairs, count, sources, spectra, below, above, lags, source_out, pair_out,
                  near, by_window, cross, sems):
    channels = spectra.shape[0]
    base = (lax.axis_index("seg") * lax.axis_size("chan") + lax.axis_index("chan")) * channels
    copies = [
        pltpu.make_async_copy(below, near.at[pl.ds(0, NEAR)], sems.at[0]),
        pltpu.make_async_copy(spectra, near.at[pl.ds(NEAR, channels)], sems.at[1]),
        pltpu.make_async_copy(above, near.at[pl.ds(NEAR + channels, NEAR)], sems.at[2]),
    ] + [
        pltpu.make_async_copy(spectra.at[:, w], by_window.at[w], sems.at[3 + w]) for w in range(WIN)
    ]
    for c in copies:
        c.start()
    for c in copies:
        c.wait()
    slots = pair_out.shape[0]

    def one_pair(slot, carry):
        left = near[pairs[2 * slot] - base + NEAR]
        right = near[pairs[2 * slot + 1] - base + NEAR]
        l_re, l_im, r_re, r_im = left[:, :NB], left[:, NB:], right[:, :NB], right[:, NB:]
        cross[pl.ds(slot, 1), :NB] = jnp.sum(l_re * r_re + l_im * r_im, axis=0, keepdims=True)
        cross[pl.ds(slot, 1), NB:] = jnp.sum(l_re * r_im - l_im * r_re, axis=0, keepdims=True)
        return carry

    lax.fori_loop(0, slots, one_pair, 0, unroll=4)
    result = dot3(cross[:slots], lags[0], lags[1])
    live = lax.broadcasted_iota(jnp.int32, (slots, 1), 0) < count[0]
    pair_out[...] = result * live.astype(jnp.float32)

    half_tiles = TILES // 2

    def one_source(s, carry):
        for t in range(half_tiles):
            re = jnp.zeros((channels, LANES), jnp.float32)
            im = jnp.zeros((channels, LANES), jnp.float32)
            for w in range(WIN):
                s_re = sources[s, t, w : w + 1]
                s_im = sources[s, half_tiles + t, w : w + 1]
                c_re = by_window[w, :, t * LANES : (t + 1) * LANES]
                c_im = by_window[w, :, NB + t * LANES : NB + (t + 1) * LANES]
                re += s_re * c_re + s_im * c_im
                im += s_re * c_im - s_im * c_re
            cross[pl.ds(s * channels, channels), t * LANES : (t + 1) * LANES] = re
            cross[pl.ds(s * channels, channels), NB + t * LANES : NB + (t + 1) * LANES] = im
        return carry

    lax.fori_loop(0, SOURCES, one_source, 0)
    source_out[...] = dot3(cross[...], lags[0], lags[1])


def shards(dims, das_records, source_ids, near_pairs, pair_count):
    xs, ys, zs = dims
    channels = das_records.shape[0]
    vmem = pl.BlockSpec(memory_space=pltpu.VMEM)
    smem = pl.BlockSpec(memory_space=pltpu.SMEM)
    hbm = pl.BlockSpec(memory_space=pl.ANY)
    f32 = jnp.float32
    spectra, kept = pl.pallas_call(
        local_kernel,
        out_shape=(
            jax.ShapeDtypeStruct((channels, WIN, 2 * NB), f32),
            jax.ShapeDtypeStruct((SOURCES, TILES, WIN, LANES), f32),
        ),
        in_specs=[smem, vmem, vmem, vmem],
        out_specs=(vmem, vmem),
        scratch_shapes=[pltpu.VMEM((16 * WIN, LPAD), f32)],
        compiler_params=pltpu.CompilerParams(vmem_limit_bytes=VMEM_LIMIT),
        name="local_spectra",
    )(source_ids.reshape(-1), das_records, jnp.asarray(band_tables()), jnp.asarray(smooth_table()))
    per_core = SOURCES // CORES
    per_rank = per_core // xs
    per_y = TILES // ys
    n_copies = 3 + 2 * (xs - 1) + 2 * (ys - 1) + (zs - 1) + xs
    tile = (WIN, LANES)
    sources, below, above = pl.pallas_call(
        functools.partial(exchange_kernel, dims),
        out_shape=(
            jax.ShapeDtypeStruct((SOURCES, TILES) + tile, f32),
            jax.ShapeDtypeStruct((NEAR, WIN, 2 * NB), f32),
            jax.ShapeDtypeStruct((NEAR, WIN, 2 * NB), f32),
        ),
        in_specs=[vmem, hbm],
        out_specs=(vmem, hbm, hbm),
        scratch_shapes=[
            pltpu.VMEM((per_core, TILES) + tile, f32),
            pltpu.VMEM((per_rank, TILES) + tile, f32),
            pltpu.VMEM((per_rank, per_y) + tile, f32),
            pltpu.VMEM((per_core, TILES) + tile, f32),
            pltpu.VMEM((xs - 1, per_rank, TILES) + tile, f32),
            pltpu.VMEM((ys - 1, per_rank, per_y) + tile, f32),
            pltpu.VMEM((zs - 1, per_rank, per_y) + tile, f32),
            pltpu.SemaphoreType.DMA((n_copies,)),
            pltpu.SemaphoreType.DMA((n_copies,)),
        ],
        compiler_params=pltpu.CompilerParams(collective_id=0, has_side_effects=True),
        name="exchange",
    )(kept, spectra)
    source_xcorr, pair_xcorr = pl.pallas_call(
        result_kernel,
        out_shape=(
            jax.ShapeDtypeStruct((SOURCES * channels, LAGS), f32),
            jax.ShapeDtypeStruct((near_pairs.shape[0], LAGS), f32),
        ),
        in_specs=[smem, smem, vmem, hbm, hbm, hbm, vmem],
        out_specs=(vmem, vmem),
        scratch_shapes=[
            pltpu.VMEM((channels + 2 * NEAR, WIN, 2 * NB), f32),
            pltpu.VMEM((WIN, channels, 2 * NB), f32),
            pltpu.VMEM((SOURCES * channels, 2 * NB), f32),
            pltpu.SemaphoreType.DMA((3 + WIN,)),
        ],
        compiler_params=pltpu.CompilerParams(vmem_limit_bytes=VMEM_LIMIT),
        name="correlate",
    )(near_pairs.reshape(-1), pair_count, sources, spectra, below, above, jnp.asarray(lag_tables()))
    return source_xcorr.reshape(source_ids.shape + (channels, LAGS)), pair_xcorr


def solution(mesh, xs=X_CHIPS):
    dims = (xs, mesh.shape["chan"] // xs, mesh.shape["seg"] // CORES)
    in_specs = (P(("seg", "chan"), None, None), P(), P(("seg", "chan"), None), P(("seg", "chan")))
    out_specs = (P(None, None, ("seg", "chan"), None), P(("seg", "chan"), None))
    return jax.shard_map(
        functools.partial(shards, dims), mesh=mesh, in_specs=in_specs, out_specs=out_specs, check_vma=False
    )
```

```python
import functools
import math

import jax
import jax.numpy as jnp
import ml_dtypes
import numpy as np
from jax import lax
from jax.experimental import pallas as pl
from jax.experimental.pallas import tpu as pltpu
from jax.sharding import PartitionSpec as P

WIN = 8
L = 1500
HALF = L // 2
LPAD = 1536
KPAD = 768
FLO = 30
NB = 512
EVEN = NB // 2
SMOOTH = 4
LAGS = 256
SOURCES = 8
NEAR = 8
ROWS = 8
LANES = 128
CORES = 2
X_CHIPS = 4

clip_level = 2.0
water_level = 0.1
epsilon = 1e-06

SMOOTH_AT = 4 * KPAD
LAG_AT = SMOOTH_AT + NB
TABLE_ROWS = LAG_AT + 2 * NB

MESH = pl.DeviceIdType.MESH
VMEM_LIMIT = 62 * 1024 * 1024


def split(table):
    high = table.astype(np.float32).astype(ml_dtypes.bfloat16)
    low = (table - high.astype(np.float64)).astype(np.float32).astype(ml_dtypes.bfloat16)
    return high, low


def bin_order():
    return np.concatenate([np.arange(0, NB, 2), np.arange(1, NB, 2)])


@functools.lru_cache(maxsize=None)
def band_tables():
    sample = np.arange(HALF)
    out = np.zeros((2, 2, KPAD, NB), ml_dtypes.bfloat16)
    for parity in range(2):
        freq = FLO + np.arange(parity, NB, 2)
        phase = (sample[:, None] * freq[None, :] % L) * (2.0 * math.pi / L)
        table = np.concatenate([np.cos(phase), -np.sin(phase)], axis=1)
        out[parity, 0, :HALF], out[parity, 1, :HALF] = split(table)
    return out


@functools.lru_cache(maxsize=None)
def lag_tables():
    freq = FLO + bin_order()
    lag = np.arange(LAGS) - LAGS // 2
    phase = (freq[:, None] * lag[None, :] % L) * (2.0 * math.pi / L)
    table = np.concatenate([np.cos(phase), -np.sin(phase)], axis=0) / math.sqrt(WIN * NB)
    return np.stack(split(table))


@functools.lru_cache(maxsize=None)
def smooth_table():
    count = np.zeros((NB, NB))
    for centre in range(NB):
        for step in range(-SMOOTH, SMOOTH + 1):
            count[min(max(centre + step, 0), NB - 1), centre] += 1
    order = bin_order()
    return count[order][:, order].astype(ml_dtypes.bfloat16)


def all_tables():
    band = band_tables().reshape(SMOOTH_AT, NB)
    lags = np.concatenate(list(lag_tables()), axis=1)
    return np.concatenate([band, smooth_table(), lags], axis=0)


def dot(a, b):
    return jnp.dot(a, b, preferred_element_type=jnp.float32)


def halves(value):
    high = value.astype(jnp.bfloat16)
    return high, (value - high.astype(jnp.float32)).astype(jnp.bfloat16)


def dot3(value, high_table, low_table):
    high, low = halves(value)
    return dot(high, high_table) + dot(low, high_table) + dot(high, low_table)


def spectra_of(records, padded, tables):
    centered = records - jnp.sum(records, axis=-1, keepdims=True) * (1.0 / L)
    power = jnp.sum(centered * centered, axis=-1, keepdims=True) * (1.0 / L)
    normed = jnp.clip(centered * (1.0 / jnp.sqrt(power + epsilon)), -clip_level, clip_level)
    padded[:, :L] = normed
    first = padded[:, :KPAD]
    second = pltpu.roll(padded[...], LPAD - HALF, 1)[:, :KPAD]
    even = dot3(first + second, tables[:KPAD], tables[KPAD : 2 * KPAD])
    odd = dot3(first - second, tables[2 * KPAD : 3 * KPAD], tables[3 * KPAD : SMOOTH_AT])
    real = jnp.concatenate([even[:, :EVEN], odd[:, :EVEN]], axis=1)
    imag = jnp.concatenate([even[:, EVEN:], odd[:, EVEN:]], axis=1)
    amplitude = jnp.sqrt(real * real + imag * imag)
    high, low = halves(amplitude)
    smooth = tables[SMOOTH_AT:LAG_AT]
    smoothed = (dot(high, smooth) + dot(low, smooth)) * (1.0 / (2 * SMOOTH + 1))
    mean = jnp.sum(amplitude, axis=-1, keepdims=True) * (water_level / NB)
    scale = 1.0 / (smoothed + mean + epsilon)
    return real * scale, imag * scale


def kernel(dims, ids, pairs, count, records_hbm, tables_hbm, source_out, pair_out,
           records, tables, padded, near, by_window, kept, half, r0, ra1, rb1, ra2, rb2,
           piece, r3, sources, acc, pair_cross, source_res, pair_res, load, send, recv):
    xs, ys, zs = dims
    seg, chan = lax.axis_index("seg"), lax.axis_index("chan")
    n_chan = lax.axis_size("chan")
    total = lax.axis_size("seg") * n_chan
    me = seg * n_chan + chan
    z, core = seg // CORES, lax.rem(seg, CORES)
    y, x = chan // xs, lax.rem(chan, xs)
    channels = records.shape[0]
    base = me * channels
    per_core = SOURCES // CORES
    group = per_core // 2
    span = WIN // ys

    loads = [pltpu.make_async_copy(records_hbm, records, load.at[0])] + [
        pltpu.make_async_copy(tables_hbm.at[lo:hi], tables.at[lo:hi], load.at[1 + k])
        for k, (lo, hi) in enumerate([(0, SMOOTH_AT), (SMOOTH_AT, LAG_AT), (LAG_AT, TABLE_ROWS)])
    ]
    for c in loads:
        c.start()

    def at(z_, core_, y_, x_):
        return (z_ * CORES + core_, y_ * xs + x_)

    def of(index):
        return (index // n_chan, lax.rem(index, n_chan))

    def at_x(d):
        return at(z, core, y, lax.rem(x + d, xs))

    def at_y(d):
        return at(z, core, lax.rem(y + d, ys), x)

    def at_z(d):
        return at(lax.rem(z + d, zs), core, y, x)

    sibling = at(z, 1 - core, y, x)
    after = of(lax.rem(me + 1, total))
    before = of(lax.rem(me + total - 1, total))

    barrier = pltpu.get_barrier_semaphore()
    greeted = [sibling, after, before]
    greeted += [at_x(d) for d in range(1, xs)]
    greeted += [at_y(d) for d in range(1, ys)]
    greeted += [at_z(d) for d in range(1, zs)]
    for device in greeted:
        pl.semaphore_signal(barrier, inc=1, device_id=device, device_id_type=MESH)

    tail = padded.shape[0]
    padded[:, LPAD - LANES :] = jnp.zeros((tail, LANES), jnp.float32)
    acc[...] = jnp.zeros_like(acc)

    loads[0].wait()
    rows = [records[jnp.clip(ids[s % 2, s // 2] - base, 0, channels - 1)] for s in range(SOURCES)]
    block = jnp.concatenate(rows, axis=0)
    loads[1].wait()
    loads[2].wait()
    real, imag = spectra_of(block, padded.at[pl.ds(0, SOURCES * WIN)], tables)
    for s in range(SOURCES):
        local = ids[s % 2, s // 2] - base
        mine = jnp.logical_and(local >= 0, local < channels).astype(jnp.float32)
        for r in range(ROWS):
            part = real if r < ROWS // 2 else imag
            lane = (r % (ROWS // 2)) * LANES
            kept[s, :, r, :] = part[s * WIN : (s + 1) * WIN, lane : lane + LANES] * mine

    used = [0]

    def slots(number):
        first = used[0]
        used[0] += number
        return first

    def remote(k, src, dst, device):
        return pltpu.make_async_remote_copy(
            src_ref=src, dst_ref=dst, send_sem=send.at[k], recv_sem=recv.at[k],
            device_id=device, device_id_type=MESH)

    def start(copies):
        for c in copies:
            c.start()
        return copies

    def arrive(copies):
        for c in copies:
            c.wait_recv()

    def spectra_to_near(places):
        block = jnp.concatenate([records[lo:hi] for lo, hi in places], axis=0)
        real, imag = spectra_of(block.reshape(-1, L), padded, tables)
        row = 0
        for lo, hi in places:
            size = hi - lo
            near[NEAR + lo : NEAR + hi, :, :NB] = real[row * WIN : (row + size) * WIN].reshape(size, WIN, NB)
            near[NEAR + lo : NEAR + hi, :, NB:] = imag[row * WIN : (row + size) * WIN].reshape(size, WIN, NB)
            row += size

    pl.semaphore_wait(barrier, len(greeted))
    k = slots(1)
    core_copy = start([remote(k, kept.at[pl.ds(per_core * (1 - core), per_core)], r0, sibling)])
    arrive(core_copy)
    half[...] = kept[pl.ds(per_core * core, per_core)] + r0[...]

    def to(d, mine, n):
        return pl.ds(lax.rem(mine + d, n) * span, span)

    ka, kb = slots(ys), slots(zs)
    first = start(
        [remote(ka + d, half.at[pl.ds(0, group), to(d, y, ys)], ra1.at[d - 1], at_y(d)) for d in range(1, ys)]
        + [remote(kb + d, half.at[pl.ds(group, group), to(d, z, zs)], rb1.at[d - 1], at_z(d)) for d in range(1, zs)])

    spectra_to_near([(0, NEAR), (channels - NEAR, channels)])
    k = slots(2)
    halo = start([
        remote(k, near.at[pl.ds(channels, NEAR)], near.at[pl.ds(0, NEAR)], after),
        remote(k + 1, near.at[pl.ds(NEAR, NEAR)], near.at[pl.ds(NEAR + channels, NEAR)], before)])
    spectra_to_near([(NEAR, channels - NEAR)])
    turned = [
        pltpu.make_async_copy(near.at[pl.ds(NEAR, channels), w], by_window.at[w], load.at[len(loads) + w])
        for w in range(WIN)
    ]
    for c in turned:
        c.start()

    arrive(first)
    piece[0] = half[:group, pl.ds(y * span, span)] + sum(ra1[d] for d in range(ys - 1))
    piece[1] = half[group:, pl.ds(z * span, span)] + sum(rb1[d] for d in range(zs - 1))
    ka, kb = slots(zs), slots(ys)
    second = start(
        [remote(ka + d, piece.at[0], ra2.at[d - 1], at_z(d)) for d in range(1, zs)]
        + [remote(kb + d, piece.at[1], rb2.at[d - 1], at_y(d)) for d in range(1, ys)])
    arrive(second)
    piece[2] = piece[0] + sum(ra2[d] for d in range(zs - 1))
    piece[3] = piece[1] + sum(rb2[d] for d in range(ys - 1))
    k = slots(xs)
    third = start([remote(k + d, piece.at[pl.ds(2, 2)], r3.at[d - 1], at_x(d)) for d in range(1, xs)])

    arrive(halo)
    slot_count = pair_cross.shape[0]

    def one_pair(slot, carry):
        left = near[jnp.clip(pairs[0, slot] - base + NEAR, 0, channels + 2 * NEAR - 1)]
        right = near[jnp.clip(pairs[1, slot] - base + NEAR, 0, channels + 2 * NEAR - 1)]
        l_re, l_im, r_re, r_im = left[:, :NB], left[:, NB:], right[:, :NB], right[:, NB:]
        pair_cross[pl.ds(slot, 1), :NB] = jnp.sum(l_re * r_re + l_im * r_im, axis=0, keepdims=True)
        pair_cross[pl.ds(slot, 1), NB:] = jnp.sum(l_re * r_im - l_im * r_re, axis=0, keepdims=True)
        return carry

    lax.fori_loop(0, slot_count, one_pair, 0, unroll=4)

    arrive(third)
    whole = piece[2:] + sum(r3[d] for d in range(xs - 1))
    own = core * per_core
    other = (1 - core) * per_core
    sources[pl.ds(own, group), pl.ds(y * span, span)] = whole[0]
    sources[pl.ds(own + group, group), pl.ds(z * span, span)] = whole[1]

    def block_a(owner, origin):
        return sources.at[pl.ds(owner, group), pl.ds(origin * span, span)]

    def block_b(owner, origin):
        return sources.at[pl.ds(owner + group, group), pl.ds(origin * span, span)]

    ka, kb, fa, fb = slots(ys), slots(zs), slots(ys), slots(zs)

    def gather_a(d):
        return remote(ka + d, block_a(own, y), block_a(own, y), at_y(d))

    def gather_b(d):
        return remote(kb + d, block_b(own, z), block_b(own, z), at_z(d))

    def pass_a(d):
        got = block_a(own, lax.rem(y + ys - d, ys))
        return remote(fa + d, got, got, sibling)

    def pass_b(d):
        got = block_b(own, lax.rem(z + zs - d, zs))
        return remote(fb + d, got, got, sibling)

    fourth = start([g(d) for d in range(1, ys) for g in (gather_a, gather_b)])
    start([pass_a(0), pass_b(0)])

    for c in loads[3:] + turned:
        c.wait()
    result = dot3(pair_cross[...], tables[LAG_AT:, :LAGS], tables[LAG_AT:, LAGS:])
    live = lax.broadcasted_iota(jnp.int32, (slot_count, 1), 0) < count[0]
    pair_res[...] = result * live.astype(jnp.float32)
    pair_store = pltpu.make_async_copy(pair_res, pair_out, load.at[0])
    pair_store.start()

    def add_window(s, w):
        for t in range(ROWS // 2):
            s_re = sources[s, w, t : t + 1]
            s_im = sources[s, w, ROWS // 2 + t : ROWS // 2 + t + 1]
            re, im = slice(t * LANES, (t + 1) * LANES), slice(NB + t * LANES, NB + (t + 1) * LANES)
            c_re = by_window[w, :, re]
            c_im = by_window[w, :, im]
            acc[s, :, re] += s_re * c_re + s_im * c_im
            acc[s, :, im] += s_re * c_im - s_im * c_re

    def add_blocks(owner, d):
        for g in range(group):
            for v in range(span):
                add_window(owner + g, lax.rem(y + ys - d, ys) * span + v)
                add_window(owner + group + g, lax.rem(z + zs - d, zs) * span + v)

    def nth(i):
        return jnp.where(lax.rem(i, 2) == 1, (i + 1) // 2, lax.rem(ys - i // 2, ys))

    add_blocks(own, 0)

    def step(i, carry):
        d, previous = nth(i), nth(i - 1)
        gather_a(d).wait_recv()
        pass_a(d).start()
        gather_b(d).wait_recv()
        pass_b(d).start()
        add_blocks(own, d)
        pass_a(previous).wait_recv()
        pass_b(previous).wait_recv()
        add_blocks(other, previous)
        return carry

    lax.fori_loop(1, ys, step, 0)
    source_res[0] = dot3(acc[pl.ds(own, per_core)].reshape(per_core * channels, 2 * NB), tables[LAG_AT:, :LAGS], tables[LAG_AT:, LAGS:])
    store_own = pltpu.make_async_copy(source_res.at[0], source_out.at[own // per_core], load.at[1])
    store_own.start()
    last = ys // 2
    pass_a(last).wait_recv()
    pass_b(last).wait_recv()
    add_blocks(other, last)
    source_res[1] = dot3(acc[pl.ds(other, per_core)].reshape(per_core * channels, 2 * NB), tables[LAG_AT:, :LAGS], tables[LAG_AT:, LAGS:])
    store_other = pltpu.make_async_copy(source_res.at[1], source_out.at[other // per_core], load.at[2])
    store_other.start()
    for c in core_copy + first + halo + second + third + fourth + [p(d) for d in range(ys) for p in (pass_a, pass_b)]:
        c.wait_send()
    pair_store.wait()
    store_own.wait()
    store_other.wait()


def shards(dims, das_records, source_ids, near_pairs, pair_count):
    xs, ys, zs = dims
    channels = das_records.shape[0]
    slot_count = near_pairs.shape[0]
    smem = pl.BlockSpec(memory_space=pltpu.SMEM)
    hbm = pl.BlockSpec(memory_space=pl.ANY)
    f32 = jnp.float32
    per_core = SOURCES // CORES
    group = per_core // 2
    span = WIN // ys
    tables = all_tables()
    tile = (ROWS, LANES)
    block = (group, span) + tile
    n_copies = 3 + 4 * ys + 4 * zs + xs
    source_xcorr, pair_xcorr = pl.pallas_call(
        functools.partial(kernel, dims),
        out_shape=(
            jax.ShapeDtypeStruct((CORES, per_core * channels, LAGS), f32),
            jax.ShapeDtypeStruct((slot_count, LAGS), f32),
        ),
        in_specs=[smem, smem, smem, hbm, hbm],
        out_specs=(hbm, hbm),
        scratch_shapes=[
            pltpu.VMEM(das_records.shape, f32),
            pltpu.VMEM(tables.shape, jnp.bfloat16),
            pltpu.VMEM((2 * NEAR * WIN, LPAD), f32),
            pltpu.VMEM((channels + 2 * NEAR, WIN, 2 * NB), f32),
            pltpu.VMEM((WIN, channels, 2 * NB), f32),
            pltpu.VMEM((SOURCES, WIN) + tile, f32),
            pltpu.VMEM((per_core, WIN) + tile, f32),
            pltpu.VMEM((per_core, WIN) + tile, f32),
            pltpu.VMEM((ys - 1,) + block, f32),
            pltpu.VMEM((zs - 1,) + block, f32),
            pltpu.VMEM((zs - 1,) + block, f32),
            pltpu.VMEM((ys - 1,) + block, f32),
            pltpu.VMEM((4,) + block, f32),
            pltpu.VMEM((xs - 1, 2) + block, f32),
            pltpu.VMEM((SOURCES, WIN) + tile, f32),
            pltpu.VMEM((SOURCES, channels, 2 * NB), f32),
            pltpu.VMEM((slot_count, 2 * NB), f32),
            pltpu.VMEM((CORES, per_core * channels, LAGS), f32),
            pltpu.VMEM((slot_count, LAGS), f32),
            pltpu.SemaphoreType.DMA((4 + WIN,)),
            pltpu.SemaphoreType.DMA((n_copies,)),
            pltpu.SemaphoreType.DMA((n_copies,)),
        ],
        compiler_params=pltpu.CompilerParams(
            collective_id=0, has_side_effects=True, vmem_limit_bytes=VMEM_LIMIT),
        name="correlate_all",
    )(source_ids.T, near_pairs.T, pair_count, das_records, jnp.asarray(tables))
    return source_xcorr.reshape(source_ids.shape + (channels, LAGS)), pair_xcorr


def solution(mesh, xs=X_CHIPS):
    dims = (xs, mesh.shape["chan"] // xs, mesh.shape["seg"] // CORES)
    in_specs = (P(("seg", "chan"), None, None), P(), P(("seg", "chan"), None), P(("seg", "chan")))
    out_specs = (P(None, None, ("seg", "chan"), None), P(("seg", "chan"), None))
    return jax.shard_map(
        functools.partial(shards, dims), mesh=mesh, in_specs=in_specs, out_specs=out_specs, check_vma=False
    )
```

```python
import functools
import math

import jax
import jax.numpy as jnp
import ml_dtypes
import numpy as np
from jax import lax
from jax.experimental import pallas as pl
from jax.experimental.pallas import tpu as pltpu
from jax.sharding import PartitionSpec as P

WIN = 8
L = 1500
HALF = L // 2
LPAD = 1536
KPAD = 768
FLO = 30
NB = 512
EVEN = NB // 2
SMOOTH = 4
LAGS = 256
SOURCES = 8
NEAR = 8
ROWS = 8
LANES = 128
CORES = 2
X_CHIPS = 4
PARTS = 2

clip_level = 2.0
water_level = 0.1
epsilon = 1e-06

SMOOTH_AT = 4 * KPAD
LAG_AT = SMOOTH_AT + NB
TABLE_ROWS = LAG_AT + 2 * NB

MESH = pl.DeviceIdType.MESH
VMEM_LIMIT = 62 * 1024 * 1024


def split(table):
    high = table.astype(np.float32).astype(ml_dtypes.bfloat16)
    low = (table - high.astype(np.float64)).astype(np.float32).astype(ml_dtypes.bfloat16)
    return high, low


def bin_order():
    return np.concatenate([np.arange(0, NB, 2), np.arange(1, NB, 2)])


@functools.lru_cache(maxsize=None)
def band_tables():
    sample = np.arange(HALF)
    out = np.zeros((2, 2, KPAD, NB), ml_dtypes.bfloat16)
    for parity in range(2):
        freq = FLO + np.arange(parity, NB, 2)
        phase = (sample[:, None] * freq[None, :] % L) * (2.0 * math.pi / L)
        table = np.concatenate([np.cos(phase), -np.sin(phase)], axis=1)
        out[parity, 0, :HALF], out[parity, 1, :HALF] = split(table)
    return out


@functools.lru_cache(maxsize=None)
def lag_tables():
    freq = FLO + bin_order()
    lag = np.arange(LAGS) - LAGS // 2
    phase = (freq[:, None] * lag[None, :] % L) * (2.0 * math.pi / L)
    table = np.concatenate([np.cos(phase), -np.sin(phase)], axis=0) / math.sqrt(WIN * NB)
    return np.stack(split(table))


@functools.lru_cache(maxsize=None)
def smooth_table():
    count = np.zeros((NB, NB))
    for centre in range(NB):
        for step in range(-SMOOTH, SMOOTH + 1):
            count[min(max(centre + step, 0), NB - 1), centre] += 1
    order = bin_order()
    return count[order][:, order].astype(ml_dtypes.bfloat16)


def all_tables():
    band = band_tables().reshape(SMOOTH_AT, NB)
    lags = np.concatenate(list(lag_tables()), axis=1)
    return np.concatenate([band, smooth_table(), lags], axis=0)


def dot(a, b):
    return jnp.dot(a, b, preferred_element_type=jnp.float32)


def halves(value):
    high = value.astype(jnp.bfloat16)
    return high, (value - high.astype(jnp.float32)).astype(jnp.bfloat16)


def dot3(value, high_table, low_table):
    high, low = halves(value)
    rows = value.shape[0]
    both = dot(jnp.concatenate([high, low], axis=0), high_table)
    return both[:rows] + both[rows:] + dot(high, low_table)


def normalize_into(records, padded):
    centered = records - jnp.sum(records, axis=-1, keepdims=True) * (1.0 / L)
    power = jnp.sum(centered * centered, axis=-1, keepdims=True) * (1.0 / L)
    normed = jnp.clip(centered * (1.0 / jnp.sqrt(power + epsilon)), -clip_level, clip_level)
    padded[:, :L] = normed


def spectra_of(padded, tables):
    first = padded[:, :KPAD]
    second = pltpu.roll(padded[...], LPAD - HALF, 1)[:, :KPAD]
    even = dot3(first + second, tables[:KPAD], tables[KPAD : 2 * KPAD])
    odd = dot3(first - second, tables[2 * KPAD : 3 * KPAD], tables[3 * KPAD : SMOOTH_AT])
    real = jnp.concatenate([even[:, :EVEN], odd[:, :EVEN]], axis=1)
    imag = jnp.concatenate([even[:, EVEN:], odd[:, EVEN:]], axis=1)
    amplitude = jnp.sqrt(real * real + imag * imag)
    high, low = halves(amplitude)
    smooth = tables[SMOOTH_AT:LAG_AT]
    rows = amplitude.shape[0]
    both = dot(jnp.concatenate([high, low], axis=0), smooth)
    smoothed = (both[:rows] + both[rows:]) * (1.0 / (2 * SMOOTH + 1))
    mean = jnp.sum(amplitude, axis=-1, keepdims=True) * (water_level / NB)
    scale = 1.0 / (smoothed + mean + epsilon)
    return real * scale, imag * scale


def far_first(n):
    return sorted(range(1, n), key=lambda d: -min(d, n - d))


def kernel(dims, ids_hbm, pairs_hbm, count_hbm, records_hbm, tables_hbm, source_out, pair_out,
           records, tables, padded, near, by_window, kept, half, r0, ra1, rb1, ra2, rb2,
           piece, r3, sources, acc, pair_cross, source_res, pair_res, ids, pairs, count, load, send, recv):
    xs, ys, zs = dims
    seg, chan = lax.axis_index("seg"), lax.axis_index("chan")
    n_chan = lax.axis_size("chan")
    total = lax.axis_size("seg") * n_chan
    me = seg * n_chan + chan
    z, core = seg // CORES, lax.rem(seg, CORES)
    y, x = chan // xs, lax.rem(chan, xs)
    channels = records.shape[0]
    base = me * channels
    per_core = SOURCES // CORES
    group = per_core // 2
    span = WIN // ys

    def at(z_, core_, y_, x_):
        return (z_ * CORES + core_, y_ * xs + x_)

    def of(index):
        return (index // n_chan, lax.rem(index, n_chan))

    def at_x(d):
        return at(z, core, y, lax.rem(x + d, xs))

    def at_y(d):
        return at(z, core, lax.rem(y + d, ys), x)

    def at_z(d):
        return at(lax.rem(z + d, zs), core, y, x)

    sibling = at(z, 1 - core, y, x)
    after = of(lax.rem(me + 1, total))
    before = of(lax.rem(me + total - 1, total))

    barrier = pltpu.get_barrier_semaphore()
    y_far, x_far = far_first(ys), far_first(xs)
    greeted = [there(d) for d in y_far for there in (at_y, at_z)]
    greeted += [at_x(d) for d in x_far] + [after, before, sibling]
    for device in greeted:
        pl.semaphore_signal(barrier, inc=1, device_id=device, device_id_type=MESH)

    numbers = [
        pltpu.make_async_copy(src, dst, load.at[4 + k])
        for k, (src, dst) in enumerate([(ids_hbm, ids), (pairs_hbm, pairs), (count_hbm, count)])
    ]
    numbers[0].start()
    loads = [pltpu.make_async_copy(records_hbm, records, load.at[0])] + [
        pltpu.make_async_copy(tables_hbm.at[lo:hi], tables.at[lo:hi], load.at[1 + k])
        for k, (lo, hi) in enumerate([(0, SMOOTH_AT), (SMOOTH_AT, LAG_AT), (LAG_AT, TABLE_ROWS)])
    ]
    for c in loads[:3] + numbers[1:]:
        c.start()

    tail = padded.shape[0]
    padded[:, LPAD - LANES :] = jnp.zeros((tail, LANES), jnp.float32)
    acc[...] = jnp.zeros_like(acc)

    numbers[0].wait()
    loads[0].wait()
    rows = [records[jnp.clip(ids[s % 2, s // 2] - base, 0, channels - 1)] for s in range(SOURCES)]
    block = jnp.concatenate(rows, axis=0)
    owned = padded.at[pl.ds(0, SOURCES * WIN)]
    normalize_into(block, owned)
    loads[1].wait()
    loads[2].wait()
    real, imag = spectra_of(owned, tables)
    for s in range(SOURCES):
        local = ids[s % 2, s // 2] - base
        mine = jnp.logical_and(local >= 0, local < channels).astype(jnp.float32)
        for r in range(ROWS):
            part = real if r < ROWS // 2 else imag
            lane = (r % (ROWS // 2)) * LANES
            kept[s, :, r, :] = part[s * WIN : (s + 1) * WIN, lane : lane + LANES] * mine

    used = [0]

    def slots(number):
        first = used[0]
        used[0] += number
        return first

    def remote(k, src, dst, device):
        return pltpu.make_async_remote_copy(
            src_ref=src, dst_ref=dst, send_sem=send.at[k], recv_sem=recv.at[k],
            device_id=device, device_id_type=MESH)

    def start(copies):
        for c in copies:
            c.start()
        return copies

    def arrive(copies):
        for c in copies:
            c.wait_recv()

    def spectra_to_near(places):
        block = jnp.concatenate([records[lo:hi] for lo, hi in places], axis=0)
        normalize_into(block.reshape(-1, L), padded)
        real, imag = spectra_of(padded, tables)
        row = 0
        for lo, hi in places:
            size = hi - lo
            near[NEAR + lo : NEAR + hi, :, :NB] = real[row * WIN : (row + size) * WIN].reshape(size, WIN, NB)
            near[NEAR + lo : NEAR + hi, :, NB:] = imag[row * WIN : (row + size) * WIN].reshape(size, WIN, NB)
            row += size

    pl.semaphore_wait(barrier, len(greeted))
    k = slots(1)
    core_copy = start([remote(k, kept.at[pl.ds(per_core * (1 - core), per_core)], r0, sibling)])
    arrive(core_copy)
    half[...] = kept[pl.ds(per_core * core, per_core)] + r0[...]

    def to(d, mine, n):
        return pl.ds(lax.rem(mine + d, n) * span, span)

    ka, kb = slots(ys), slots(zs)
    first = start(
        [c for d in y_far for c in (
            remote(ka + d, half.at[pl.ds(0, group), to(d, y, ys)], ra1.at[d - 1], at_y(d)),
            remote(kb + d, half.at[pl.ds(group, group), to(d, z, zs)], rb1.at[d - 1], at_z(d)))])
    loads[3].start()

    spectra_to_near([(0, NEAR), (channels - NEAR, channels)])
    k = slots(2)
    halo = start([
        remote(k, near.at[pl.ds(channels, NEAR)], near.at[pl.ds(0, NEAR)], after),
        remote(k + 1, near.at[pl.ds(NEAR, NEAR)], near.at[pl.ds(NEAR + channels, NEAR)], before)])
    spectra_to_near([(NEAR, channels - NEAR)])
    turned = [
        pltpu.make_async_copy(near.at[pl.ds(NEAR, channels), w], by_window.at[w], load.at[7 + w])
        for w in range(WIN)
    ]
    for c in turned:
        c.start()

    arrive(first)
    piece[0] = half[:group, pl.ds(y * span, span)] + sum(ra1[d] for d in range(ys - 1))
    piece[1] = half[group:, pl.ds(z * span, span)] + sum(rb1[d] for d in range(zs - 1))
    ka, kb = slots(zs), slots(ys)
    second = start(
        [c for d in y_far for c in (
            remote(ka + d, piece.at[0], ra2.at[d - 1], at_z(d)),
            remote(kb + d, piece.at[1], rb2.at[d - 1], at_y(d)))])
    arrive(second)
    piece[2] = piece[0] + sum(ra2[d] for d in range(zs - 1))
    piece[3] = piece[1] + sum(rb2[d] for d in range(ys - 1))
    k = slots(xs)
    third = start([remote(k + d, piece.at[pl.ds(2, 2)], r3.at[d - 1], at_x(d)) for d in x_far])

    arrive(halo)
    numbers[1].wait()
    slot_count = pair_cross.shape[0]

    def one_pair(slot, carry):
        left = near[jnp.clip(pairs[0, slot] - base + NEAR, 0, channels + 2 * NEAR - 1)]
        right = near[jnp.clip(pairs[1, slot] - base + NEAR, 0, channels + 2 * NEAR - 1)]
        l_re, l_im, r_re, r_im = left[:, :NB], left[:, NB:], right[:, :NB], right[:, NB:]
        pair_cross[pl.ds(slot, 1), :NB] = jnp.sum(l_re * r_re + l_im * r_im, axis=0, keepdims=True)
        pair_cross[pl.ds(slot, 1), NB:] = jnp.sum(l_re * r_im - l_im * r_re, axis=0, keepdims=True)
        return carry

    lax.fori_loop(0, slot_count, one_pair, 0, unroll=4)

    arrive(third)
    whole = piece[2:] + sum(r3[d] for d in range(xs - 1))
    own = core * per_core
    other = (1 - core) * per_core
    sources[pl.ds(own, group), pl.ds(y * span, span)] = whole[0]
    sources[pl.ds(own + group, group), pl.ds(z * span, span)] = whole[1]

    def block_a(owner, origin):
        return sources.at[pl.ds(owner, group), pl.ds(origin * span, span)]

    def block_b(owner, origin):
        return sources.at[pl.ds(owner + group, group), pl.ds(origin * span, span)]

    ka, kb, fa, fb = slots(ys), slots(zs), slots(ys), slots(zs)

    def gather_a(d):
        return remote(ka + d, block_a(own, y), block_a(own, y), at_y(d))

    def gather_b(d):
        return remote(kb + d, block_b(own, z), block_b(own, z), at_z(d))

    def pass_a(d):
        got = block_a(own, lax.rem(y + ys - d, ys))
        return remote(fa + d, got, got, sibling)

    def pass_b(d):
        got = block_b(own, lax.rem(z + zs - d, zs))
        return remote(fb + d, got, got, sibling)

    fourth = start([g(d) for d in y_far for g in (gather_a, gather_b)])
    start([pass_a(0), pass_b(0)])

    for c in loads[3:] + turned:
        c.wait()
    numbers[2].wait()
    result = dot3(pair_cross[...], tables[LAG_AT:, :LAGS], tables[LAG_AT:, LAGS:])
    live = lax.broadcasted_iota(jnp.int32, (slot_count, 1), 0) < count[0]
    pair_res[...] = result * live.astype(jnp.float32)
    pair_store = pltpu.make_async_copy(pair_res, pair_out, load.at[0])
    pair_store.start()

    def add_window(s, w):
        for t in range(ROWS // 2):
            s_re = sources[s, w, t : t + 1]
            s_im = sources[s, w, ROWS // 2 + t : ROWS // 2 + t + 1]
            re, im = slice(t * LANES, (t + 1) * LANES), slice(NB + t * LANES, NB + (t + 1) * LANES)
            c_re = by_window[w, :, re]
            c_im = by_window[w, :, im]
            acc[s, :, re] += s_re * c_re + s_im * c_im
            acc[s, :, im] += s_re * c_im - s_im * c_re

    def add_blocks(owner, d):
        for g in range(group):
            for v in range(span):
                add_window(owner + g, lax.rem(y + ys - d, ys) * span + v)
                add_window(owner + group + g, lax.rem(z + zs - d, zs) * span + v)

    def nth(i):
        return jnp.where(lax.rem(i, 2) == 1, (i + 1) // 2, lax.rem(ys - i // 2, ys))

    add_blocks(own, 0)

    def step(i, carry):
        d, previous = nth(i), nth(i - 1)
        gather_a(d).wait_recv()
        pass_a(d).start()
        gather_b(d).wait_recv()
        pass_b(d).start()
        add_blocks(own, d)
        pass_a(previous).wait_recv()
        pass_b(previous).wait_recv()
        add_blocks(other, previous)
        return carry

    lax.fori_loop(1, ys, step, 0)
    source_res[0] = dot3(acc[pl.ds(own, per_core)].reshape(per_core * channels, 2 * NB), tables[LAG_AT:, :LAGS], tables[LAG_AT:, LAGS:])
    store_own = pltpu.make_async_copy(source_res.at[0], source_out.at[own // per_core], load.at[1])
    store_own.start()
    last = ys // 2
    pass_a(last).wait_recv()
    pass_b(last).wait_recv()
    add_blocks(other, last)
    source_res[1] = dot3(acc[pl.ds(other, per_core)].reshape(per_core * channels, 2 * NB), tables[LAG_AT:, :LAGS], tables[LAG_AT:, LAGS:])
    store_other = pltpu.make_async_copy(source_res.at[1], source_out.at[other // per_core], load.at[2])
    store_other.start()
    for c in core_copy + first + halo + second + third + fourth + [p(d) for d in range(ys) for p in (pass_a, pass_b)]:
        c.wait_send()
    pair_store.wait()
    store_own.wait()
    store_other.wait()


def deliver(source_in, pair_in, source_out, pair_out, source_held, pair_held, sems):
    inward, outward = [], []
    for src, held, dst in ((source_in, source_held, source_out), (pair_in, pair_held, pair_out)):
        rows = src.shape[0] // PARTS
        for p in range(PARTS):
            part = pl.ds(p * rows, rows)
            k = len(inward)
            inward.append(pltpu.make_async_copy(src.at[part], held.at[part], sems.at[0, k]))
            outward.append(pltpu.make_async_copy(held.at[part], dst.at[part], sems.at[1, k]))
    for c in inward:
        c.start()
    for c, o in zip(inward, outward):
        c.wait()
        o.start()
    for o in outward:
        o.wait()


def shards(dims, das_records, source_ids, near_pairs, pair_count):
    xs, ys, zs = dims
    channels = das_records.shape[0]
    slot_count = near_pairs.shape[0]
    hbm = pl.BlockSpec(memory_space=pl.ANY)
    f32 = jnp.float32
    per_core = SOURCES // CORES
    group = per_core // 2
    span = WIN // ys
    tables = all_tables()
    tile = (ROWS, LANES)
    block = (group, span) + tile
    n_copies = 3 + 4 * ys + 4 * zs + xs
    source_xcorr, pair_xcorr = pl.pallas_call(
        functools.partial(kernel, dims),
        out_shape=(
            jax.ShapeDtypeStruct((CORES, per_core * channels, LAGS), f32),
            jax.ShapeDtypeStruct((slot_count, LAGS), f32),
        ),
        in_specs=[hbm, hbm, hbm, hbm, hbm],
        out_specs=(hbm, hbm),
        scratch_shapes=[
            pltpu.VMEM(das_records.shape, f32),
            pltpu.VMEM(tables.shape, jnp.bfloat16),
            pltpu.VMEM((2 * NEAR * WIN, LPAD), f32),
            pltpu.VMEM((channels + 2 * NEAR, WIN, 2 * NB), f32),
            pltpu.VMEM((WIN, channels, 2 * NB), f32),
            pltpu.VMEM((SOURCES, WIN) + tile, f32),
            pltpu.VMEM((per_core, WIN) + tile, f32),
            pltpu.VMEM((per_core, WIN) + tile, f32),
            pltpu.VMEM((ys - 1,) + block, f32),
            pltpu.VMEM((zs - 1,) + block, f32),
            pltpu.VMEM((zs - 1,) + block, f32),
            pltpu.VMEM((ys - 1,) + block, f32),
            pltpu.VMEM((4,) + block, f32),
            pltpu.VMEM((xs - 1, 2) + block, f32),
            pltpu.VMEM((SOURCES, WIN) + tile, f32),
            pltpu.VMEM((SOURCES, channels, 2 * NB), f32),
            pltpu.VMEM((slot_count, 2 * NB), f32),
            pltpu.VMEM((CORES, per_core * channels, LAGS), f32),
            pltpu.VMEM((slot_count, LAGS), f32),
            pltpu.SMEM(source_ids.shape[::-1], jnp.int32),
            pltpu.SMEM(near_pairs.shape[::-1], jnp.int32),
            pltpu.SMEM(pair_count.shape, jnp.int32),
            pltpu.SemaphoreType.DMA((7 + WIN,)),
            pltpu.SemaphoreType.DMA((n_copies,)),
            pltpu.SemaphoreType.DMA((n_copies,)),
        ],
        compiler_params=pltpu.CompilerParams(
            collective_id=0, has_side_effects=True, vmem_limit_bytes=VMEM_LIMIT),
        name="correlate_all",
    )(source_ids.T, near_pairs.T, pair_count, das_records, jnp.asarray(tables))
    source_xcorr, pair_xcorr = pl.pallas_call(
        deliver,
        out_shape=(
            jax.ShapeDtypeStruct(source_xcorr.shape, f32),
            jax.ShapeDtypeStruct(pair_xcorr.shape, f32),
        ),
        in_specs=[hbm, hbm],
        out_specs=(hbm, hbm),
        scratch_shapes=[
            pltpu.VMEM(source_xcorr.shape, f32),
            pltpu.VMEM(pair_xcorr.shape, f32),
            pltpu.SemaphoreType.DMA((2, 2 * PARTS)),
        ],
        compiler_params=pltpu.CompilerParams(vmem_limit_bytes=VMEM_LIMIT),
        name="deliver",
    )(source_xcorr, pair_xcorr)
    return source_xcorr.reshape(source_ids.shape + (channels, LAGS)), pair_xcorr


def solution(mesh, xs=X_CHIPS):
    dims = (xs, mesh.shape["chan"] // xs, mesh.shape["seg"] // CORES)
    in_specs = (P(("seg", "chan"), None, None), P(), P(("seg", "chan"), None), P(("seg", "chan")))
    out_specs = (P(None, None, ("seg", "chan"), None), P(("seg", "chan"), None))
    return jax.shard_map(
        functools.partial(shards, dims), mesh=mesh, in_specs=in_specs, out_specs=out_specs, check_vma=False
    )
```

```python
import functools
import math

import jax
import jax.numpy as jnp
import ml_dtypes
import numpy as np
from jax import lax
from jax.experimental import pallas as pl
from jax.experimental.pallas import tpu as pltpu
from jax.sharding import PartitionSpec as P

WIN = 8
L = 1500
HALF = L // 2
LPAD = 1536
KPAD = 768
FLO = 30
NB = 512
EVEN = NB // 2
SMOOTH = 4
LAGS = 256
SOURCES = 8
NEAR = 8
ROWS = 8
LANES = 128
CORES = 2
X_CHIPS = 4
PARTS = 2

clip_level = 2.0
water_level = 0.1
epsilon = 1e-06

SMOOTH_AT = 4 * KPAD
LAG_AT = SMOOTH_AT + NB
TABLE_ROWS = LAG_AT + 2 * NB

MESH = pl.DeviceIdType.MESH
VMEM_LIMIT = 62 * 1024 * 1024


def split(table):
    high = table.astype(np.float32).astype(ml_dtypes.bfloat16)
    low = (table - high.astype(np.float64)).astype(np.float32).astype(ml_dtypes.bfloat16)
    return high, low


def bin_order():
    return np.concatenate([np.arange(0, NB, 2), np.arange(1, NB, 2)])


@functools.lru_cache(maxsize=None)
def band_tables():
    sample = np.arange(HALF)
    out = np.zeros((2, 2, KPAD, NB), ml_dtypes.bfloat16)
    for parity in range(2):
        freq = FLO + np.arange(parity, NB, 2)
        phase = (sample[:, None] * freq[None, :] % L) * (2.0 * math.pi / L)
        table = np.concatenate([np.cos(phase), -np.sin(phase)], axis=1)
        out[parity, 0, :HALF], out[parity, 1, :HALF] = split(table)
    return out


@functools.lru_cache(maxsize=None)
def lag_tables():
    freq = FLO + bin_order()
    lag = np.arange(LAGS) - LAGS // 2
    phase = (freq[:, None] * lag[None, :] % L) * (2.0 * math.pi / L)
    table = np.concatenate([np.cos(phase), -np.sin(phase)], axis=0) / math.sqrt(WIN * NB)
    return np.stack(split(table))


@functools.lru_cache(maxsize=None)
def smooth_table():
    count = np.zeros((NB, NB))
    for centre in range(NB):
        for step in range(-SMOOTH, SMOOTH + 1):
            count[min(max(centre + step, 0), NB - 1), centre] += 1
    order = bin_order()
    return count[order][:, order].astype(ml_dtypes.bfloat16)


def all_tables():
    band = band_tables().reshape(SMOOTH_AT, NB)
    lags = np.concatenate(list(lag_tables()), axis=1)
    return np.concatenate([band, smooth_table(), lags], axis=0)


def dot(a, b):
    return jnp.dot(a, b, preferred_element_type=jnp.float32)


def halves(value):
    high = value.astype(jnp.bfloat16)
    return high, (value - high.astype(jnp.float32)).astype(jnp.bfloat16)


def dot3(value, high_table, low_table):
    high, low = halves(value)
    rows = value.shape[0]
    both = dot(jnp.concatenate([high, low], axis=0), high_table)
    return both[:rows] + both[rows:] + dot(high, low_table)


def normalize_into(records, padded):
    centered = records - jnp.sum(records, axis=-1, keepdims=True) * (1.0 / L)
    power = jnp.sum(centered * centered, axis=-1, keepdims=True) * (1.0 / L)
    normed = jnp.clip(centered * (1.0 / jnp.sqrt(power + epsilon)), -clip_level, clip_level)
    padded[:, :L] = normed


def spectra_of(padded, tables):
    first = padded[:, :KPAD]
    second = pltpu.roll(padded[...], LPAD - HALF, 1)[:, :KPAD]
    even = dot3(first + second, tables[:KPAD], tables[KPAD : 2 * KPAD])
    odd = dot3(first - second, tables[2 * KPAD : 3 * KPAD], tables[3 * KPAD : SMOOTH_AT])
    real = jnp.concatenate([even[:, :EVEN], odd[:, :EVEN]], axis=1)
    imag = jnp.concatenate([even[:, EVEN:], odd[:, EVEN:]], axis=1)
    amplitude = jnp.sqrt(real * real + imag * imag)
    high, low = halves(amplitude)
    smooth = tables[SMOOTH_AT:LAG_AT]
    rows = amplitude.shape[0]
    both = dot(jnp.concatenate([high, low], axis=0), smooth)
    smoothed = (both[:rows] + both[rows:]) * (1.0 / (2 * SMOOTH + 1))
    mean = jnp.sum(amplitude, axis=-1, keepdims=True) * (water_level / NB)
    scale = 1.0 / (smoothed + mean + epsilon)
    return real * scale, imag * scale


def far_first(n):
    return sorted(range(1, n), key=lambda d: -min(d, n - d))


def kernel(dims, ids_hbm, pairs_hbm, count_hbm, records_hbm, tables_hbm, source_out, pair_out,
           records, tables, padded, near, by_window, kept, half, r0, ra1, rb1, ra2, rb2,
           piece, r3, sources, acc, pair_cross, source_res, pair_res, ids, pairs, count, load, send, recv):
    xs, ys, zs = dims
    seg, chan = lax.axis_index("seg"), lax.axis_index("chan")
    n_chan = lax.axis_size("chan")
    total = lax.axis_size("seg") * n_chan
    me = seg * n_chan + chan
    z, core = seg // CORES, lax.rem(seg, CORES)
    y, x = chan // xs, lax.rem(chan, xs)
    channels = records.shape[0]
    base = me * channels
    per_core = SOURCES // CORES
    group = per_core // 2
    span = WIN // ys

    def at(z_, core_, y_, x_):
        return (z_ * CORES + core_, y_ * xs + x_)

    def of(index):
        return (index // n_chan, lax.rem(index, n_chan))

    def at_x(d):
        return at(z, core, y, lax.rem(x + d, xs))

    def at_x_other(d):
        return at(z, 1 - core, y, lax.rem(x + d, xs))

    def at_y(d):
        return at(z, core, lax.rem(y + d, ys), x)

    def at_z(d):
        return at(lax.rem(z + d, zs), core, y, x)

    sibling = at(z, 1 - core, y, x)
    after = of(lax.rem(me + 1, total))
    before = of(lax.rem(me + total - 1, total))

    barrier = pltpu.get_barrier_semaphore()
    y_far, x_far = far_first(ys), far_first(xs)
    greeted = [there(d) for d in y_far for there in (at_y, at_z)]
    greeted += [there(d) for d in x_far for there in (at_x, at_x_other)] + [after, before, sibling]
    for device in greeted:
        pl.semaphore_signal(barrier, inc=1, device_id=device, device_id_type=MESH)

    numbers = [
        pltpu.make_async_copy(src, dst, load.at[4 + k])
        for k, (src, dst) in enumerate([(ids_hbm, ids), (pairs_hbm, pairs), (count_hbm, count)])
    ]
    numbers[0].start()
    loads = [pltpu.make_async_copy(records_hbm, records, load.at[0])] + [
        pltpu.make_async_copy(tables_hbm.at[lo:hi], tables.at[lo:hi], load.at[1 + k])
        for k, (lo, hi) in enumerate([(0, SMOOTH_AT), (SMOOTH_AT, LAG_AT), (LAG_AT, TABLE_ROWS)])
    ]
    for c in loads[:3] + numbers[1:]:
        c.start()

    tail = padded.shape[0]
    padded[:, LPAD - LANES :] = jnp.zeros((tail, LANES), jnp.float32)
    acc[...] = jnp.zeros_like(acc)

    numbers[0].wait()
    loads[0].wait()
    rows = [records[jnp.clip(ids[s % 2, s // 2] - base, 0, channels - 1)] for s in range(SOURCES)]
    block = jnp.concatenate(rows, axis=0)
    owned = padded.at[pl.ds(0, SOURCES * WIN)]
    normalize_into(block, owned)
    loads[1].wait()
    loads[2].wait()
    real, imag = spectra_of(owned, tables)
    for s in range(SOURCES):
        local = ids[s % 2, s // 2] - base
        mine = jnp.logical_and(local >= 0, local < channels).astype(jnp.float32)
        for r in range(ROWS):
            part = real if r < ROWS // 2 else imag
            lane = (r % (ROWS // 2)) * LANES
            kept[s, :, r, :] = part[s * WIN : (s + 1) * WIN, lane : lane + LANES] * mine

    used = [0]

    def slots(number):
        first = used[0]
        used[0] += number
        return first

    def remote(k, src, dst, device):
        return pltpu.make_async_remote_copy(
            src_ref=src, dst_ref=dst, send_sem=send.at[k], recv_sem=recv.at[k],
            device_id=device, device_id_type=MESH)

    def start(copies):
        for c in copies:
            c.start()
        return copies

    def arrive(copies):
        for c in copies:
            c.wait_recv()

    def spectra_to_near(places):
        block = jnp.concatenate([records[lo:hi] for lo, hi in places], axis=0)
        normalize_into(block.reshape(-1, L), padded)
        real, imag = spectra_of(padded, tables)
        row = 0
        for lo, hi in places:
            size = hi - lo
            near[NEAR + lo : NEAR + hi, :, :NB] = real[row * WIN : (row + size) * WIN].reshape(size, WIN, NB)
            near[NEAR + lo : NEAR + hi, :, NB:] = imag[row * WIN : (row + size) * WIN].reshape(size, WIN, NB)
            row += size

    pl.semaphore_wait(barrier, len(greeted))
    k = slots(1)
    core_copy = start([remote(k, kept.at[pl.ds(per_core * (1 - core), per_core)], r0, sibling)])
    arrive(core_copy)
    half[...] = kept[pl.ds(per_core * core, per_core)] + r0[...]

    def to(d, mine, n):
        return pl.ds(lax.rem(mine + d, n) * span, span)

    ka, kb = slots(ys), slots(zs)
    first = start(
        [c for d in y_far for c in (
            remote(ka + d, half.at[pl.ds(0, group), to(d, y, ys)], ra1.at[d - 1], at_y(d)),
            remote(kb + d, half.at[pl.ds(group, group), to(d, z, zs)], rb1.at[d - 1], at_z(d)))])
    loads[3].start()

    spectra_to_near([(0, NEAR), (channels - NEAR, channels)])
    k = slots(2)
    halo = start([
        remote(k, near.at[pl.ds(channels, NEAR)], near.at[pl.ds(0, NEAR)], after),
        remote(k + 1, near.at[pl.ds(NEAR, NEAR)], near.at[pl.ds(NEAR + channels, NEAR)], before)])
    spectra_to_near([(NEAR, channels - NEAR)])
    turned = [
        pltpu.make_async_copy(near.at[pl.ds(NEAR, channels), w], by_window.at[w], load.at[7 + w])
        for w in range(WIN)
    ]
    for c in turned:
        c.start()

    arrive(first)
    piece[0] = half[:group, pl.ds(y * span, span)] + sum(ra1[d] for d in range(ys - 1))
    piece[1] = half[group:, pl.ds(z * span, span)] + sum(rb1[d] for d in range(zs - 1))
    ka, kb = slots(zs), slots(ys)
    second = start(
        [c for d in y_far for c in (
            remote(ka + d, piece.at[0], ra2.at[d - 1], at_z(d)),
            remote(kb + d, piece.at[1], rb2.at[d - 1], at_y(d)))])
    arrive(second)
    piece[2] = piece[0] + sum(ra2[d] for d in range(zs - 1))
    piece[3] = piece[1] + sum(rb2[d] for d in range(ys - 1))
    k = slots(2 * xs)
    summed = piece.at[pl.ds(2, 2)]
    third = start(
        [c for d in x_far for c in (
            remote(k + xs + d, summed, r3.at[1, d], at_x_other(d)), remote(k + d, summed, r3.at[0, d], at_x(d)))]
        + [remote(k + xs, summed, r3.at[1, 0], sibling)])

    arrive(halo)
    numbers[1].wait()
    slot_count = pair_cross.shape[0]

    def one_pair(slot, carry):
        left = near[jnp.clip(pairs[0, slot] - base + NEAR, 0, channels + 2 * NEAR - 1)]
        right = near[jnp.clip(pairs[1, slot] - base + NEAR, 0, channels + 2 * NEAR - 1)]
        l_re, l_im, r_re, r_im = left[:, :NB], left[:, NB:], right[:, :NB], right[:, NB:]
        pair_cross[pl.ds(slot, 1), :NB] = jnp.sum(l_re * r_re + l_im * r_im, axis=0, keepdims=True)
        pair_cross[pl.ds(slot, 1), NB:] = jnp.sum(l_re * r_im - l_im * r_re, axis=0, keepdims=True)
        return carry

    lax.fori_loop(0, slot_count, one_pair, 0, unroll=4)

    arrive(third)
    for c, whole in ((core, piece[2:] + sum(r3[0, d] for d in range(1, xs))), (1 - core, sum(r3[1, d] for d in range(xs)))):
        sources[c, 0, :, pl.ds(y * span, span)] = whole[0]
        sources[c, 1, :, pl.ds(z * span, span)] = whole[1]
    ka, kb = slots(ys), slots(zs)

    def gather_a(d):
        block = sources.at[:, 0, :, pl.ds(y * span, span)]
        return remote(ka + d, block, block, at_y(d))

    def gather_b(d):
        block = sources.at[:, 1, :, pl.ds(z * span, span)]
        return remote(kb + d, block, block, at_z(d))

    fourth = start([g(d) for d in y_far for g in (gather_a, gather_b)])

    for c in loads[3:] + turned:
        c.wait()
    numbers[2].wait()
    result = dot3(pair_cross[...], tables[LAG_AT:, :LAGS], tables[LAG_AT:, LAGS:])
    live = lax.broadcasted_iota(jnp.int32, (slot_count, 1), 0) < count[0]
    pair_res[...] = result * live.astype(jnp.float32)
    pair_store = pltpu.make_async_copy(pair_res, pair_out, load.at[0])
    pair_store.start()

    def add_window(c, h, g, w):
        s = (c * 2 + h) * group + g
        for t in range(ROWS // 2):
            s_re = sources[c, h, g, w, t : t + 1]
            s_im = sources[c, h, g, w, ROWS // 2 + t : ROWS // 2 + t + 1]
            re, im = slice(t * LANES, (t + 1) * LANES), slice(NB + t * LANES, NB + (t + 1) * LANES)
            c_re = by_window[w, :, re]
            c_im = by_window[w, :, im]
            acc[s, :, re] += s_re * c_re + s_im * c_im
            acc[s, :, im] += s_re * c_im - s_im * c_re

    def add_blocks(d):
        for v in range(span):
            for h, w in enumerate((lax.rem(y + ys - d, ys) * span + v, lax.rem(z + zs - d, zs) * span + v)):
                for c in range(CORES):
                    for g in range(group):
                        add_window(c, h, g, w)

    def nth(i):
        return jnp.where(lax.rem(i, 2) == 1, (i + 1) // 2, lax.rem(ys - i // 2, ys))

    add_blocks(0)

    def step(i, carry):
        d = nth(i)
        gather_a(d).wait_recv()
        gather_b(d).wait_recv()
        add_blocks(d)
        return carry

    lax.fori_loop(1, ys, step, 0)
    stores = []
    for c in range(CORES):
        mine = acc[c * per_core : (c + 1) * per_core].reshape(per_core * channels, 2 * NB)
        source_res[c] = dot3(mine, tables[LAG_AT:, :LAGS], tables[LAG_AT:, LAGS:])
        stores.append(pltpu.make_async_copy(source_res.at[c], source_out.at[c], load.at[1 + c]))
        stores[c].start()
    for c in core_copy + first + halo + second + third + fourth:
        c.wait_send()
    pair_store.wait()
    for c in stores:
        c.wait()


def deliver(source_in, pair_in, source_out, pair_out, source_held, pair_held, sems):
    inward, outward = [], []
    for src, held, dst in ((source_in, source_held, source_out), (pair_in, pair_held, pair_out)):
        rows = src.shape[0] // PARTS
        for p in range(PARTS):
            part = pl.ds(p * rows, rows)
            k = len(inward)
            inward.append(pltpu.make_async_copy(src.at[part], held.at[part], sems.at[0, k]))
            outward.append(pltpu.make_async_copy(held.at[part], dst.at[part], sems.at[1, k]))
    for c in inward:
        c.start()
    for c, o in zip(inward, outward):
        c.wait()
        o.start()
    for o in outward:
        o.wait()


def shards(dims, das_records, source_ids, near_pairs, pair_count):
    xs, ys, zs = dims
    channels = das_records.shape[0]
    slot_count = near_pairs.shape[0]
    hbm = pl.BlockSpec(memory_space=pl.ANY)
    f32 = jnp.float32
    per_core = SOURCES // CORES
    group = per_core // 2
    span = WIN // ys
    tables = all_tables()
    tile = (ROWS, LANES)
    block = (group, span) + tile
    n_copies = 3 + 3 * ys + 3 * zs + 2 * xs
    source_xcorr, pair_xcorr = pl.pallas_call(
        functools.partial(kernel, dims),
        out_shape=(
            jax.ShapeDtypeStruct((CORES, per_core * channels, LAGS), f32),
            jax.ShapeDtypeStruct((slot_count, LAGS), f32),
        ),
        in_specs=[hbm, hbm, hbm, hbm, hbm],
        out_specs=(hbm, hbm),
        scratch_shapes=[
            pltpu.VMEM(das_records.shape, f32),
            pltpu.VMEM(tables.shape, jnp.bfloat16),
            pltpu.VMEM((2 * NEAR * WIN, LPAD), f32),
            pltpu.VMEM((channels + 2 * NEAR, WIN, 2 * NB), f32),
            pltpu.VMEM((WIN, channels, 2 * NB), f32),
            pltpu.VMEM((SOURCES, WIN) + tile, f32),
            pltpu.VMEM((per_core, WIN) + tile, f32),
            pltpu.VMEM((per_core, WIN) + tile, f32),
            pltpu.VMEM((ys - 1,) + block, f32),
            pltpu.VMEM((zs - 1,) + block, f32),
            pltpu.VMEM((zs - 1,) + block, f32),
            pltpu.VMEM((ys - 1,) + block, f32),
            pltpu.VMEM((4,) + block, f32),
            pltpu.VMEM((2, xs, 2) + block, f32),
            pltpu.VMEM((CORES, 2, group, WIN) + tile, f32),
            pltpu.VMEM((SOURCES, channels, 2 * NB), f32),
            pltpu.VMEM((slot_count, 2 * NB), f32),
            pltpu.VMEM((CORES, per_core * channels, LAGS), f32),
            pltpu.VMEM((slot_count, LAGS), f32),
            pltpu.SMEM(source_ids.shape[::-1], jnp.int32),
            pltpu.SMEM(near_pairs.shape[::-1], jnp.int32),
            pltpu.SMEM(pair_count.shape, jnp.int32),
            pltpu.SemaphoreType.DMA((7 + WIN,)),
            pltpu.SemaphoreType.DMA((n_copies,)),
            pltpu.SemaphoreType.DMA((n_copies,)),
        ],
        compiler_params=pltpu.CompilerParams(
            collective_id=0, has_side_effects=True, vmem_limit_bytes=VMEM_LIMIT),
        name="correlate_all",
    )(source_ids.T, near_pairs.T, pair_count, das_records, jnp.asarray(tables))
    source_xcorr, pair_xcorr = pl.pallas_call(
        deliver,
        out_shape=(
            jax.ShapeDtypeStruct(source_xcorr.shape, f32),
            jax.ShapeDtypeStruct(pair_xcorr.shape, f32),
        ),
        in_specs=[hbm, hbm],
        out_specs=(hbm, hbm),
        scratch_shapes=[
            pltpu.VMEM(source_xcorr.shape, f32),
            pltpu.VMEM(pair_xcorr.shape, f32),
            pltpu.SemaphoreType.DMA((2, 2 * PARTS)),
        ],
        compiler_params=pltpu.CompilerParams(vmem_limit_bytes=VMEM_LIMIT),
        name="deliver",
    )(source_xcorr, pair_xcorr)
    return source_xcorr.reshape(source_ids.shape + (channels, LAGS)), pair_xcorr


def solution(mesh, xs=X_CHIPS):
    dims = (xs, mesh.shape["chan"] // xs, mesh.shape["seg"] // CORES)
    in_specs = (P(("seg", "chan"), None, None), P(), P(("seg", "chan"), None), P(("seg", "chan")))
    out_specs = (P(None, None, ("seg", "chan"), None), P(("seg", "chan"), None))
    return jax.shard_map(
        functools.partial(shards, dims), mesh=mesh, in_specs=in_specs, out_specs=out_specs, check_vma=False
    )
```

```python
import functools
import math

import jax
import jax.numpy as jnp
import ml_dtypes
import numpy as np
from jax import lax
from jax.experimental import pallas as pl
from jax.experimental.pallas import tpu as pltpu
from jax.sharding import PartitionSpec as P

WIN = 8
L = 1500
HALF = L // 2
LPAD = 1536
KPAD = 768
FLO = 30
NB = 512
EVEN = NB // 2
SMOOTH = 4
LAGS = 256
SOURCES = 8
NEAR = 8
ROWS = 8
LANES = 128
CORES = 2
X_CHIPS = 4
PARTS = 2

clip_level = 2.0
water_level = 0.1
epsilon = 1e-06

SMOOTH_AT = 4 * KPAD
LAG_AT = SMOOTH_AT + NB
TABLE_ROWS = LAG_AT + 2 * NB

MESH = pl.DeviceIdType.MESH
VMEM_LIMIT = 62 * 1024 * 1024


def split(table):
    high = table.astype(np.float32).astype(ml_dtypes.bfloat16)
    low = (table - high.astype(np.float64)).astype(np.float32).astype(ml_dtypes.bfloat16)
    return high, low


def bin_order():
    return np.concatenate([np.arange(0, NB, 2), np.arange(1, NB, 2)])


@functools.lru_cache(maxsize=None)
def band_tables():
    sample = np.arange(HALF)
    out = np.zeros((2, 2, KPAD, NB), ml_dtypes.bfloat16)
    for parity in range(2):
        freq = FLO + np.arange(parity, NB, 2)
        phase = (sample[:, None] * freq[None, :] % L) * (2.0 * math.pi / L)
        table = np.concatenate([np.cos(phase), -np.sin(phase)], axis=1)
        out[parity, 0, :HALF], out[parity, 1, :HALF] = split(table)
    return out


@functools.lru_cache(maxsize=None)
def lag_tables():
    freq = FLO + bin_order()
    lag = np.arange(LAGS) - LAGS // 2
    phase = (freq[:, None] * lag[None, :] % L) * (2.0 * math.pi / L)
    table = np.concatenate([np.cos(phase), -np.sin(phase)], axis=0) / math.sqrt(WIN * NB)
    return np.stack(split(table))


@functools.lru_cache(maxsize=None)
def smooth_table():
    count = np.zeros((NB, NB))
    for centre in range(NB):
        for step in range(-SMOOTH, SMOOTH + 1):
            count[min(max(centre + step, 0), NB - 1), centre] += 1
    order = bin_order()
    return count[order][:, order].astype(ml_dtypes.bfloat16)


def all_tables():
    band = band_tables().reshape(SMOOTH_AT, NB)
    lags = np.concatenate(list(lag_tables()), axis=1)
    return np.concatenate([band, smooth_table(), lags], axis=0)


def dot(a, b):
    return jnp.dot(a, b, preferred_element_type=jnp.float32)


def halves(value):
    high = value.astype(jnp.bfloat16)
    return high, (value - high.astype(jnp.float32)).astype(jnp.bfloat16)


def dot3(value, high_table, low_table):
    high, low = halves(value)
    rows = value.shape[0]
    both = dot(jnp.concatenate([high, low], axis=0), high_table)
    return both[:rows] + both[rows:] + dot(high, low_table)


def normalize_into(records, padded):
    centered = records - jnp.sum(records, axis=-1, keepdims=True) * (1.0 / L)
    power = jnp.sum(centered * centered, axis=-1, keepdims=True) * (1.0 / L)
    normed = jnp.clip(centered * (1.0 / jnp.sqrt(power + epsilon)), -clip_level, clip_level)
    padded[:, :L] = normed


def spectra_of(padded, tables):
    first = padded[:, :KPAD]
    second = pltpu.roll(padded[...], LPAD - HALF, 1)[:, :KPAD]
    even = dot3(first + second, tables[:KPAD], tables[KPAD : 2 * KPAD])
    odd = dot3(first - second, tables[2 * KPAD : 3 * KPAD], tables[3 * KPAD : SMOOTH_AT])
    real = jnp.concatenate([even[:, :EVEN], odd[:, :EVEN]], axis=1)
    imag = jnp.concatenate([even[:, EVEN:], odd[:, EVEN:]], axis=1)
    amplitude = jnp.sqrt(real * real + imag * imag)
    high, low = halves(amplitude)
    smooth = tables[SMOOTH_AT:LAG_AT]
    rows = amplitude.shape[0]
    both = dot(jnp.concatenate([high, low], axis=0), smooth)
    smoothed = (both[:rows] + both[rows:]) * (1.0 / (2 * SMOOTH + 1))
    mean = jnp.sum(amplitude, axis=-1, keepdims=True) * (water_level / NB)
    scale = 1.0 / (smoothed + mean + epsilon)
    return real * scale, imag * scale


def far_first(n):
    return sorted(range(1, n), key=lambda d: -min(d, n - d))


def kernel(dims, ids_hbm, pairs_hbm, count_hbm, records_hbm, tables_hbm, source_out, pair_out,
           records, tables, padded, near, by_window, kept, half, r0, ra1, rb1, ra2, rb2,
           piece, r3, sources, acc, pair_cross, source_res, pair_res, ids, pairs, count, load, send, recv):
    xs, ys, zs = dims
    seg, chan = lax.axis_index("seg"), lax.axis_index("chan")
    n_chan = lax.axis_size("chan")
    total = lax.axis_size("seg") * n_chan
    me = seg * n_chan + chan
    z, core = seg // CORES, lax.rem(seg, CORES)
    y, x = chan // xs, lax.rem(chan, xs)
    channels = records.shape[0]
    base = me * channels
    per_core = SOURCES // CORES
    group = per_core // 2
    span = WIN // ys

    def at(z_, core_, y_, x_):
        return (z_ * CORES + core_, y_ * xs + x_)

    def of(index):
        return (index // n_chan, lax.rem(index, n_chan))

    def at_x(d):
        return at(z, core, y, lax.rem(x + d, xs))

    def at_x_other(d):
        return at(z, 1 - core, y, lax.rem(x + d, xs))

    def at_y(d):
        return at(z, core, lax.rem(y + d, ys), x)

    def at_z(d):
        return at(lax.rem(z + d, zs), core, y, x)

    sibling = at(z, 1 - core, y, x)
    after = of(lax.rem(me + 1, total))
    before = of(lax.rem(me + total - 1, total))

    barrier = pltpu.get_barrier_semaphore()
    y_far, x_far = far_first(ys), far_first(xs)
    greeted = [there(d) for d in y_far for there in (at_y, at_z)]
    greeted += [there(d) for d in x_far for there in (at_x, at_x_other)] + [after, before, sibling]
    for device in greeted:
        pl.semaphore_signal(barrier, inc=1, device_id=device, device_id_type=MESH)

    numbers = [
        pltpu.make_async_copy(src, dst, load.at[4 + k])
        for k, (src, dst) in enumerate([(ids_hbm, ids), (pairs_hbm, pairs), (count_hbm, count)])
    ]
    numbers[0].start()
    loads = [pltpu.make_async_copy(records_hbm, records, load.at[0])] + [
        pltpu.make_async_copy(tables_hbm.at[lo:hi], tables.at[lo:hi], load.at[1 + k])
        for k, (lo, hi) in enumerate([(0, SMOOTH_AT), (SMOOTH_AT, LAG_AT), (LAG_AT, TABLE_ROWS)])
    ]
    for c in loads[:3] + numbers[1:]:
        c.start()

    tail = padded.shape[0]
    padded[:, LPAD - LANES :] = jnp.zeros((tail, LANES), jnp.float32)
    acc[...] = jnp.zeros_like(acc)

    numbers[0].wait()
    loads[0].wait()
    rows = [records[jnp.clip(ids[s % 2, s // 2] - base, 0, channels - 1)] for s in range(SOURCES)]
    block = jnp.concatenate(rows, axis=0)
    owned = padded.at[pl.ds(0, SOURCES * WIN)]
    normalize_into(block, owned)
    loads[1].wait()
    loads[2].wait()
    real, imag = spectra_of(owned, tables)
    for s in range(SOURCES):
        local = ids[s % 2, s // 2] - base
        mine = jnp.logical_and(local >= 0, local < channels).astype(jnp.float32)
        for r in range(ROWS):
            part = real if r < ROWS // 2 else imag
            lane = (r % (ROWS // 2)) * LANES
            kept[s, :, r, :] = part[s * WIN : (s + 1) * WIN, lane : lane + LANES] * mine

    used = [0]

    def slots(number):
        first = used[0]
        used[0] += number
        return first

    def remote(k, src, dst, device):
        return pltpu.make_async_remote_copy(
            src_ref=src, dst_ref=dst, send_sem=send.at[k], recv_sem=recv.at[k],
            device_id=device, device_id_type=MESH)

    def start(copies):
        for c in copies:
            c.start()
        return copies

    def arrive(copies):
        for c in copies:
            c.wait_recv()

    def spectra_to_near(places):
        block = jnp.concatenate([records[lo:hi] for lo, hi in places], axis=0)
        normalize_into(block.reshape(-1, L), padded)
        real, imag = spectra_of(padded, tables)
        row = 0
        for lo, hi in places:
            size = hi - lo
            near[NEAR + lo : NEAR + hi, :, :NB] = real[row * WIN : (row + size) * WIN].reshape(size, WIN, NB)
            near[NEAR + lo : NEAR + hi, :, NB:] = imag[row * WIN : (row + size) * WIN].reshape(size, WIN, NB)
            row += size

    pl.semaphore_wait(barrier, len(greeted))
    k = slots(1)
    core_copy = start([remote(k, kept.at[pl.ds(per_core * (1 - core), per_core)], r0, sibling)])
    arrive(core_copy)
    half[...] = kept[pl.ds(per_core * core, per_core)] + r0[...]

    def to(d, mine, n):
        return pl.ds(lax.rem(mine + d, n) * span, span)

    ka, kb = slots(ys), slots(zs)
    first = start(
        [c for d in y_far for c in (
            remote(ka + d, half.at[pl.ds(0, group), to(d, y, ys)], ra1.at[d - 1], at_y(d)),
            remote(kb + d, half.at[pl.ds(group, group), to(d, z, zs)], rb1.at[d - 1], at_z(d)))])
    loads[3].start()

    spectra_to_near([(0, NEAR), (channels - NEAR, channels)])
    k_halo = slots(4)

    def halo_part(p):
        size = NEAR // 2
        up, down = channels + p * size, NEAR + p * size
        return start([
            remote(k_halo + 2 * p, near.at[pl.ds(up, size)], near.at[pl.ds(up - channels, size)], after),
            remote(k_halo + 2 * p + 1, near.at[pl.ds(down, size)], near.at[pl.ds(down + channels, size)], before)])

    halo = halo_part(0)
    spectra_to_near([(NEAR, channels - NEAR)])
    turned = [
        pltpu.make_async_copy(near.at[pl.ds(NEAR, channels), w], by_window.at[w], load.at[7 + w])
        for w in range(WIN)
    ]
    for c in turned:
        c.start()

    arrive(first)
    piece[0] = half[:group, pl.ds(y * span, span)] + sum(ra1[d] for d in range(ys - 1))
    piece[1] = half[group:, pl.ds(z * span, span)] + sum(rb1[d] for d in range(zs - 1))
    ka, kb = slots(zs), slots(ys)
    second = start(
        [c for d in y_far for c in (
            remote(ka + d, piece.at[0], ra2.at[d - 1], at_z(d)),
            remote(kb + d, piece.at[1], rb2.at[d - 1], at_y(d)))])
    halo += halo_part(1)
    arrive(second)
    piece[2] = piece[0] + sum(ra2[d] for d in range(zs - 1))
    piece[3] = piece[1] + sum(rb2[d] for d in range(ys - 1))
    k = slots(2 * xs)
    summed = piece.at[pl.ds(2, 2)]
    third = start(
        [c for d in x_far for c in (
            remote(k + xs + d, summed, r3.at[1, d], at_x_other(d)), remote(k + d, summed, r3.at[0, d], at_x(d)))]
        + [remote(k + xs, summed, r3.at[1, 0], sibling)])

    arrive(halo)
    numbers[1].wait()
    slot_count = pair_cross.shape[0]

    def one_pair(slot, carry):
        left = near[jnp.clip(pairs[0, slot] - base + NEAR, 0, channels + 2 * NEAR - 1)]
        right = near[jnp.clip(pairs[1, slot] - base + NEAR, 0, channels + 2 * NEAR - 1)]
        l_re, l_im, r_re, r_im = left[:, :NB], left[:, NB:], right[:, :NB], right[:, NB:]
        pair_cross[pl.ds(slot, 1), :NB] = jnp.sum(l_re * r_re + l_im * r_im, axis=0, keepdims=True)
        pair_cross[pl.ds(slot, 1), NB:] = jnp.sum(l_re * r_im - l_im * r_re, axis=0, keepdims=True)
        return carry

    lax.fori_loop(0, slot_count, one_pair, 0, unroll=4)

    arrive(third)
    for c, whole in ((core, piece[2:] + sum(r3[0, d] for d in range(1, xs))), (1 - core, sum(r3[1, d] for d in range(xs)))):
        sources[c, 0, :, pl.ds(y * span, span)] = whole[0]
        sources[c, 1, :, pl.ds(z * span, span)] = whole[1]
    ka, kb = slots(ys), slots(zs)

    def gather_a(d):
        block = sources.at[:, 0, :, pl.ds(y * span, span)]
        return remote(ka + d, block, block, at_y(d))

    def gather_b(d):
        block = sources.at[:, 1, :, pl.ds(z * span, span)]
        return remote(kb + d, block, block, at_z(d))

    fourth = start([g(d) for d in y_far for g in (gather_a, gather_b)])

    for c in loads[3:] + turned:
        c.wait()
    numbers[2].wait()
    result = dot3(pair_cross[...], tables[LAG_AT:, :LAGS], tables[LAG_AT:, LAGS:])
    live = lax.broadcasted_iota(jnp.int32, (slot_count, 1), 0) < count[0]
    pair_res[...] = result * live.astype(jnp.float32)
    pair_store = pltpu.make_async_copy(pair_res, pair_out, load.at[0])
    pair_store.start()

    def add_blocks(*distances):
        for h, (mine, n) in enumerate(((y, ys), (z, zs))):
            windows = [lax.rem(mine + n - d, n) * span + v for d in distances for v in range(span)]
            for t in range(ROWS // 2):
                re, im = slice(t * LANES, (t + 1) * LANES), slice(NB + t * LANES, NB + (t + 1) * LANES)
                local = [(by_window[w, :, re], by_window[w, :, im]) for w in windows]
                for c in range(CORES):
                    for g in range(group):
                        s = (c * 2 + h) * group + g
                        sum_re, sum_im = acc[s, :, re], acc[s, :, im]
                        for w, (c_re, c_im) in zip(windows, local):
                            s_re = sources[c, h, g, w, t : t + 1]
                            s_im = sources[c, h, g, w, ROWS // 2 + t : ROWS // 2 + t + 1]
                            sum_re += s_re * c_re + s_im * c_im
                            sum_im += s_re * c_im - s_im * c_re
                        acc[s, :, re] = sum_re
                        acc[s, :, im] = sum_im

    add_blocks(0)

    def step(i, carry):
        for d in (i, ys - i):
            gather_a(d).wait_recv()
            gather_b(d).wait_recv()
        add_blocks(i, ys - i)
        return carry

    lax.fori_loop(1, ys // 2, step, 0)
    gather_a(ys // 2).wait_recv()
    gather_b(ys // 2).wait_recv()
    add_blocks(ys // 2)
    stores = []
    for c in range(CORES):
        mine = acc[c * per_core : (c + 1) * per_core].reshape(per_core * channels, 2 * NB)
        source_res[c] = dot3(mine, tables[LAG_AT:, :LAGS], tables[LAG_AT:, LAGS:])
        stores.append(pltpu.make_async_copy(source_res.at[c], source_out.at[c], load.at[1 + c]))
        stores[c].start()
    for c in core_copy + first + halo + second + third + fourth:
        c.wait_send()
    pair_store.wait()
    for c in stores:
        c.wait()


def deliver(source_in, pair_in, source_out, pair_out, source_held, pair_held, sems):
    inward, outward = [], []
    for src, held, dst in ((source_in, source_held, source_out), (pair_in, pair_held, pair_out)):
        rows = src.shape[0] // PARTS
        for p in range(PARTS):
            part = pl.ds(p * rows, rows)
            k = len(inward)
            inward.append(pltpu.make_async_copy(src.at[part], held.at[part], sems.at[0, k]))
            outward.append(pltpu.make_async_copy(held.at[part], dst.at[part], sems.at[1, k]))
    for c in inward:
        c.start()
    for c, o in zip(inward, outward):
        c.wait()
        o.start()
    for o in outward:
        o.wait()


def shards(dims, das_records, source_ids, near_pairs, pair_count):
    xs, ys, zs = dims
    channels = das_records.shape[0]
    slot_count = near_pairs.shape[0]
    hbm = pl.BlockSpec(memory_space=pl.ANY)
    f32 = jnp.float32
    per_core = SOURCES // CORES
    group = per_core // 2
    span = WIN // ys
    tables = all_tables()
    tile = (ROWS, LANES)
    block = (group, span) + tile
    n_copies = 5 + 3 * ys + 3 * zs + 2 * xs
    source_xcorr, pair_xcorr = pl.pallas_call(
        functools.partial(kernel, dims),
        out_shape=(
            jax.ShapeDtypeStruct((CORES, per_core * channels, LAGS), f32),
            jax.ShapeDtypeStruct((slot_count, LAGS), f32),
        ),
        in_specs=[hbm, hbm, hbm, hbm, hbm],
        out_specs=(hbm, hbm),
        scratch_shapes=[
            pltpu.VMEM(das_records.shape, f32),
            pltpu.VMEM(tables.shape, jnp.bfloat16),
            pltpu.VMEM((2 * NEAR * WIN, LPAD), f32),
            pltpu.VMEM((channels + 2 * NEAR, WIN, 2 * NB), f32),
            pltpu.VMEM((WIN, channels, 2 * NB), f32),
            pltpu.VMEM((SOURCES, WIN) + tile, f32),
            pltpu.VMEM((per_core, WIN) + tile, f32),
            pltpu.VMEM((per_core, WIN) + tile, f32),
            pltpu.VMEM((ys - 1,) + block, f32),
            pltpu.VMEM((zs - 1,) + block, f32),
            pltpu.VMEM((zs - 1,) + block, f32),
            pltpu.VMEM((ys - 1,) + block, f32),
            pltpu.VMEM((4,) + block, f32),
            pltpu.VMEM((2, xs, 2) + block, f32),
            pltpu.VMEM((CORES, 2, group, WIN) + tile, f32),
            pltpu.VMEM((SOURCES, channels, 2 * NB), f32),
            pltpu.VMEM((slot_count, 2 * NB), f32),
            pltpu.VMEM((CORES, per_core * channels, LAGS), f32),
            pltpu.VMEM((slot_count, LAGS), f32),
            pltpu.SMEM(source_ids.shape[::-1], jnp.int32),
            pltpu.SMEM(near_pairs.shape[::-1], jnp.int32),
            pltpu.SMEM(pair_count.shape, jnp.int32),
            pltpu.SemaphoreType.DMA((7 + WIN,)),
            pltpu.SemaphoreType.DMA((n_copies,)),
            pltpu.SemaphoreType.DMA((n_copies,)),
        ],
        compiler_params=pltpu.CompilerParams(
            collective_id=0, has_side_effects=True, vmem_limit_bytes=VMEM_LIMIT),
        name="correlate_all",
    )(source_ids.T, near_pairs.T, pair_count, das_records, jnp.asarray(tables))
    source_xcorr, pair_xcorr = pl.pallas_call(
        deliver,
        out_shape=(
            jax.ShapeDtypeStruct(source_xcorr.shape, f32),
            jax.ShapeDtypeStruct(pair_xcorr.shape, f32),
        ),
        in_specs=[hbm, hbm],
        out_specs=(hbm, hbm),
        scratch_shapes=[
            pltpu.VMEM(source_xcorr.shape, f32),
            pltpu.VMEM(pair_xcorr.shape, f32),
            pltpu.SemaphoreType.DMA((2, 2 * PARTS)),
        ],
        compiler_params=pltpu.CompilerParams(vmem_limit_bytes=VMEM_LIMIT),
        name="deliver",
    )(source_xcorr, pair_xcorr)
    return source_xcorr.reshape(source_ids.shape + (channels, LAGS)), pair_xcorr


def solution(mesh, xs=X_CHIPS):
    dims = (xs, mesh.shape["chan"] // xs, mesh.shape["seg"] // CORES)
    in_specs = (P(("seg", "chan"), None, None), P(), P(("seg", "chan"), None), P(("seg", "chan")))
    out_specs = (P(None, None, ("seg", "chan"), None), P(("seg", "chan"), None))
    return jax.shard_map(
        functools.partial(shards, dims), mesh=mesh, in_specs=in_specs, out_specs=out_specs, check_vma=False
    )
```

```python
import functools
import math

import jax
import jax.numpy as jnp
import ml_dtypes
import numpy as np
from jax import lax
from jax.experimental import pallas as pl
from jax.experimental.pallas import tpu as pltpu
from jax.sharding import PartitionSpec as P

WIN = 8
L = 1500
HALF = L // 2
LPAD = 1536
KPAD = 768
FLO = 30
NB = 512
EVEN = NB // 2
SMOOTH = 4
LAGS = 256
SOURCES = 8
NEAR = 8
ROWS = 8
LANES = 128
CORES = 2
X_CHIPS = 4
PARTS = 2

clip_level = 2.0
water_level = 0.1
epsilon = 1e-06

SMOOTH_AT = 4 * KPAD
LAG_AT = SMOOTH_AT + NB
TABLE_ROWS = LAG_AT + 2 * NB

MESH = pl.DeviceIdType.MESH
VMEM_LIMIT = 62 * 1024 * 1024


def split(table):
    high = table.astype(np.float32).astype(ml_dtypes.bfloat16)
    low = (table - high.astype(np.float64)).astype(np.float32).astype(ml_dtypes.bfloat16)
    return high, low


def bin_order():
    return np.concatenate([np.arange(0, NB, 2), np.arange(1, NB, 2)])


@functools.lru_cache(maxsize=None)
def band_tables():
    sample = np.arange(HALF)
    out = np.zeros((2, 2, KPAD, NB), ml_dtypes.bfloat16)
    for parity in range(2):
        freq = FLO + np.arange(parity, NB, 2)
        phase = (sample[:, None] * freq[None, :] % L) * (2.0 * math.pi / L)
        table = np.concatenate([np.cos(phase), -np.sin(phase)], axis=1)
        out[parity, 0, :HALF], out[parity, 1, :HALF] = split(table)
    return out


@functools.lru_cache(maxsize=None)
def lag_tables():
    freq = FLO + bin_order()
    lag = np.arange(LAGS) - LAGS // 2
    phase = (freq[:, None] * lag[None, :] % L) * (2.0 * math.pi / L)
    table = np.concatenate([np.cos(phase), -np.sin(phase)], axis=0) / math.sqrt(WIN * NB)
    return np.stack(split(table))


@functools.lru_cache(maxsize=None)
def smooth_table():
    count = np.zeros((NB, NB))
    for centre in range(NB):
        for step in range(-SMOOTH, SMOOTH + 1):
            count[min(max(centre + step, 0), NB - 1), centre] += 1
    order = bin_order()
    return count[order][:, order].astype(ml_dtypes.bfloat16)


def all_tables():
    band = band_tables().reshape(SMOOTH_AT, NB)
    lags = np.concatenate(list(lag_tables()), axis=1)
    return np.concatenate([band, smooth_table(), lags], axis=0)


def dot(a, b):
    return jnp.dot(a, b, preferred_element_type=jnp.float32)


def halves(value):
    high = value.astype(jnp.bfloat16)
    return high, (value - high.astype(jnp.float32)).astype(jnp.bfloat16)


def dot3(value, high_table, low_table):
    high, low = halves(value)
    rows = value.shape[0]
    both = dot(jnp.concatenate([high, low], axis=0), high_table)
    return both[:rows] + both[rows:] + dot(high, low_table)


def normalize_into(records, padded):
    centered = records - jnp.sum(records, axis=-1, keepdims=True) * (1.0 / L)
    power = jnp.sum(centered * centered, axis=-1, keepdims=True) * (1.0 / L)
    normed = jnp.clip(centered * (1.0 / jnp.sqrt(power + epsilon)), -clip_level, clip_level)
    padded[:, :L] = normed


def spectra_of(padded, tables):
    first = padded[:, :KPAD]
    second = pltpu.roll(padded[...], LPAD - HALF, 1)[:, :KPAD]
    even = dot3(first + second, tables[:KPAD], tables[KPAD : 2 * KPAD])
    odd = dot3(first - second, tables[2 * KPAD : 3 * KPAD], tables[3 * KPAD : SMOOTH_AT])
    real = jnp.concatenate([even[:, :EVEN], odd[:, :EVEN]], axis=1)
    imag = jnp.concatenate([even[:, EVEN:], odd[:, EVEN:]], axis=1)
    amplitude = jnp.sqrt(real * real + imag * imag)
    high, low = halves(amplitude)
    smooth = tables[SMOOTH_AT:LAG_AT]
    rows = amplitude.shape[0]
    both = dot(jnp.concatenate([high, low], axis=0), smooth)
    smoothed = (both[:rows] + both[rows:]) * (1.0 / (2 * SMOOTH + 1))
    mean = jnp.sum(amplitude, axis=-1, keepdims=True) * (water_level / NB)
    scale = 1.0 / (smoothed + mean + epsilon)
    return real * scale, imag * scale


def far_first(n):
    return sorted(range(1, n), key=lambda d: -min(d, n - d))


def kernel(dims, ids_hbm, pairs_hbm, count_hbm, records_hbm, tables_hbm, source_out, pair_out,
           records, tables, padded, near, by_window, kept, half, r0, ra1, rb1, ra2, rb2,
           piece, r3, sources, acc, pair_cross, source_res, pair_res, ids, pairs, count, load, send, recv):
    xs, ys, zs = dims
    seg, chan = lax.axis_index("seg"), lax.axis_index("chan")
    n_chan = lax.axis_size("chan")
    total = lax.axis_size("seg") * n_chan
    me = seg * n_chan + chan
    z, core = seg // CORES, lax.rem(seg, CORES)
    y, x = chan // xs, lax.rem(chan, xs)
    channels = records.shape[0]
    base = me * channels
    per_core = SOURCES // CORES
    group = per_core // 2
    span = WIN // ys

    def at(z_, core_, y_, x_):
        return (z_ * CORES + core_, y_ * xs + x_)

    def of(index):
        return (index // n_chan, lax.rem(index, n_chan))

    def at_x(d):
        return at(z, core, y, lax.rem(x + d, xs))

    def at_x_other(d):
        return at(z, 1 - core, y, lax.rem(x + d, xs))

    def at_y(d):
        return at(z, core, lax.rem(y + d, ys), x)

    def at_z(d):
        return at(lax.rem(z + d, zs), core, y, x)

    sibling = at(z, 1 - core, y, x)
    after = of(lax.rem(me + 1, total))
    before = of(lax.rem(me + total - 1, total))

    barrier = pltpu.get_barrier_semaphore()
    y_far, x_far = far_first(ys), far_first(xs)
    greeted = [there(d) for d in y_far for there in (at_y, at_z)]
    greeted += [there(d) for d in x_far for there in (at_x, at_x_other)] + [after, before, sibling]
    for device in greeted:
        pl.semaphore_signal(barrier, inc=1, device_id=device, device_id_type=MESH)

    numbers = [
        pltpu.make_async_copy(src, dst, load.at[4 + k])
        for k, (src, dst) in enumerate([(ids_hbm, ids), (pairs_hbm, pairs), (count_hbm, count)])
    ]
    numbers[0].start()
    loads = [pltpu.make_async_copy(records_hbm, records, load.at[0])] + [
        pltpu.make_async_copy(tables_hbm.at[lo:hi], tables.at[lo:hi], load.at[1 + k])
        for k, (lo, hi) in enumerate([(0, SMOOTH_AT), (SMOOTH_AT, LAG_AT), (LAG_AT, TABLE_ROWS)])
    ]
    for c in loads[:3] + numbers[1:]:
        c.start()

    tail = padded.shape[0]
    padded[:, LPAD - LANES :] = jnp.zeros((tail, LANES), jnp.float32)

    numbers[0].wait()
    loads[0].wait()
    rows = [records[jnp.clip(ids[s % 2, s // 2] - base, 0, channels - 1)] for s in range(SOURCES)]
    block = jnp.concatenate(rows, axis=0)
    owned = padded.at[pl.ds(0, SOURCES * WIN)]
    normalize_into(block, owned)
    loads[1].wait()
    loads[2].wait()
    real, imag = spectra_of(owned, tables)
    for s in range(SOURCES):
        local = ids[s % 2, s // 2] - base
        mine = jnp.logical_and(local >= 0, local < channels).astype(jnp.float32)
        for r in range(ROWS):
            part = real if r < ROWS // 2 else imag
            lane = (r % (ROWS // 2)) * LANES
            kept[s, :, r, :] = part[s * WIN : (s + 1) * WIN, lane : lane + LANES] * mine

    used = [0]

    def slots(number):
        first = used[0]
        used[0] += number
        return first

    def remote(k, src, dst, device):
        return pltpu.make_async_remote_copy(
            src_ref=src, dst_ref=dst, send_sem=send.at[k], recv_sem=recv.at[k],
            device_id=device, device_id_type=MESH)

    def start(copies):
        for c in copies:
            c.start()
        return copies

    def arrive(copies):
        for c in copies:
            c.wait_recv()

    def spectra_to_near(places):
        block = jnp.concatenate([records[lo:hi] for lo, hi in places], axis=0)
        normalize_into(block.reshape(-1, L), padded)
        real, imag = spectra_of(padded, tables)
        row = 0
        for lo, hi in places:
            size = hi - lo
            near[NEAR + lo : NEAR + hi, :, :NB] = real[row * WIN : (row + size) * WIN].reshape(size, WIN, NB)
            near[NEAR + lo : NEAR + hi, :, NB:] = imag[row * WIN : (row + size) * WIN].reshape(size, WIN, NB)
            row += size

    pl.semaphore_wait(barrier, len(greeted))
    k = slots(1)
    core_copy = start([remote(k, kept.at[pl.ds(per_core * (1 - core), per_core)], r0, sibling)])
    arrive(core_copy)
    half[...] = kept[pl.ds(per_core * core, per_core)] + r0[...]

    def to(d, mine, n):
        return pl.ds(lax.rem(mine + d, n) * span, span)

    ka, kb = slots(ys), slots(zs)
    first = start(
        [c for d in y_far for c in (
            remote(ka + d, half.at[pl.ds(0, group), to(d, y, ys)], ra1.at[d - 1], at_y(d)),
            remote(kb + d, half.at[pl.ds(group, group), to(d, z, zs)], rb1.at[d - 1], at_z(d)))])
    loads[3].start()
    acc[...] = jnp.zeros_like(acc)

    spectra_to_near([(0, NEAR), (channels - NEAR, channels)])
    k_halo = slots(4)

    def halo_part(p):
        size = NEAR // 2
        up, down = channels + p * size, NEAR + p * size
        return start([
            remote(k_halo + 2 * p, near.at[pl.ds(up, size)], near.at[pl.ds(up - channels, size)], after),
            remote(k_halo + 2 * p + 1, near.at[pl.ds(down, size)], near.at[pl.ds(down + channels, size)], before)])

    halo = halo_part(0)
    spectra_to_near([(NEAR, channels - NEAR)])
    turned = [
        pltpu.make_async_copy(near.at[pl.ds(NEAR, channels), w], by_window.at[w], load.at[7 + w])
        for w in range(WIN)
    ]
    for c in turned:
        c.start()

    arrive(first)
    piece[0] = half[:group, pl.ds(y * span, span)] + sum(ra1[d] for d in range(ys - 1))
    piece[1] = half[group:, pl.ds(z * span, span)] + sum(rb1[d] for d in range(zs - 1))
    ka, kb = slots(zs), slots(ys)
    second = start(
        [c for d in y_far for c in (
            remote(ka + d, piece.at[0], ra2.at[d - 1], at_z(d)),
            remote(kb + d, piece.at[1], rb2.at[d - 1], at_y(d)))])
    halo += halo_part(1)
    arrive(second)
    piece[2] = piece[0] + sum(ra2[d] for d in range(zs - 1))
    piece[3] = piece[1] + sum(rb2[d] for d in range(ys - 1))
    k = slots(2 * xs)
    summed = piece.at[pl.ds(2, 2)]
    third = start(
        [c for d in x_far for c in (
            remote(k + xs + d, summed, r3.at[1, d], at_x_other(d)), remote(k + d, summed, r3.at[0, d], at_x(d)))]
        + [remote(k + xs, summed, r3.at[1, 0], sibling)])

    arrive(halo)
    numbers[1].wait()
    slot_count = pair_cross.shape[0]

    def one_pair(slot, carry):
        left = near[jnp.clip(pairs[0, slot] - base + NEAR, 0, channels + 2 * NEAR - 1)]
        right = near[jnp.clip(pairs[1, slot] - base + NEAR, 0, channels + 2 * NEAR - 1)]
        l_re, l_im, r_re, r_im = left[:, :NB], left[:, NB:], right[:, :NB], right[:, NB:]
        pair_cross[pl.ds(slot, 1), :NB] = jnp.sum(l_re * r_re + l_im * r_im, axis=0, keepdims=True)
        pair_cross[pl.ds(slot, 1), NB:] = jnp.sum(l_re * r_im - l_im * r_re, axis=0, keepdims=True)
        return carry

    lax.fori_loop(0, slot_count, one_pair, 0, unroll=4)

    arrive(third)
    for c, whole in ((core, piece[2:] + sum(r3[0, d] for d in range(1, xs))), (1 - core, sum(r3[1, d] for d in range(xs)))):
        sources[c, 0, :, pl.ds(y * span, span)] = whole[0]
        sources[c, 1, :, pl.ds(z * span, span)] = whole[1]
    ka, kb = slots(ys), slots(zs)

    def gather_a(d):
        block = sources.at[:, 0, :, pl.ds(y * span, span)]
        return remote(ka + d, block, block, at_y(d))

    def gather_b(d):
        block = sources.at[:, 1, :, pl.ds(z * span, span)]
        return remote(kb + d, block, block, at_z(d))

    fourth = start([g(d) for d in y_far for g in (gather_a, gather_b)])

    for c in loads[3:] + turned:
        c.wait()
    numbers[2].wait()
    result = dot3(pair_cross[...], tables[LAG_AT:, :LAGS], tables[LAG_AT:, LAGS:])
    live = lax.broadcasted_iota(jnp.int32, (slot_count, 1), 0) < count[0]
    pair_res[...] = result * live.astype(jnp.float32)
    pair_store = pltpu.make_async_copy(pair_res, pair_out, load.at[0])
    pair_store.start()

    def add_blocks(*distances):
        for h, (mine, n) in enumerate(((y, ys), (z, zs))):
            windows = [lax.rem(mine + n - d, n) * span + v for d in distances for v in range(span)]
            for t in range(ROWS // 2):
                re, im = slice(t * LANES, (t + 1) * LANES), slice(NB + t * LANES, NB + (t + 1) * LANES)
                local = [(by_window[w, :, re], by_window[w, :, im]) for w in windows]
                for c in range(CORES):
                    for g in range(group):
                        s = (c * 2 + h) * group + g
                        sum_re, sum_im = acc[s, :, re], acc[s, :, im]
                        for w, (c_re, c_im) in zip(windows, local):
                            s_re = sources[c, h, g, w, t : t + 1]
                            s_im = sources[c, h, g, w, ROWS // 2 + t : ROWS // 2 + t + 1]
                            sum_re += s_re * c_re + s_im * c_im
                            sum_im += s_re * c_im - s_im * c_re
                        acc[s, :, re] = sum_re
                        acc[s, :, im] = sum_im

    add_blocks(0)

    def step(i, carry):
        for d in (i, ys - i):
            gather_a(d).wait_recv()
            gather_b(d).wait_recv()
        add_blocks(i, ys - i)
        return carry

    lax.fori_loop(1, ys // 2, step, 0)
    gather_a(ys // 2).wait_recv()
    gather_b(ys // 2).wait_recv()
    add_blocks(ys // 2)
    stores = []
    for c in range(CORES):
        mine = acc[c * per_core : (c + 1) * per_core].reshape(per_core * channels, 2 * NB)
        source_res[c] = dot3(mine, tables[LAG_AT:, :LAGS], tables[LAG_AT:, LAGS:])
        stores.append(pltpu.make_async_copy(source_res.at[c], source_out.at[c], load.at[1 + c]))
        stores[c].start()
    for c in core_copy + first + halo + second + third + fourth:
        c.wait_send()
    pair_store.wait()
    for c in stores:
        c.wait()


def deliver(source_in, pair_in, source_out, pair_out, source_held, pair_held, sems):
    inward, outward = [], []
    for src, held, dst in ((source_in, source_held, source_out), (pair_in, pair_held, pair_out)):
        rows = src.shape[0] // PARTS
        for p in range(PARTS):
            part = pl.ds(p * rows, rows)
            k = len(inward)
            inward.append(pltpu.make_async_copy(src.at[part], held.at[part], sems.at[0, k]))
            outward.append(pltpu.make_async_copy(held.at[part], dst.at[part], sems.at[1, k]))
    for c in inward:
        c.start()
    for c, o in zip(inward, outward):
        c.wait()
        o.start()
    for o in outward:
        o.wait()


def shards(dims, das_records, source_ids, near_pairs, pair_count):
    xs, ys, zs = dims
    channels = das_records.shape[0]
    slot_count = near_pairs.shape[0]
    hbm = pl.BlockSpec(memory_space=pl.ANY)
    f32 = jnp.float32
    per_core = SOURCES // CORES
    group = per_core // 2
    span = WIN // ys
    tables = all_tables()
    tile = (ROWS, LANES)
    block = (group, span) + tile
    n_copies = 5 + 3 * ys + 3 * zs + 2 * xs
    source_xcorr, pair_xcorr = pl.pallas_call(
        functools.partial(kernel, dims),
        out_shape=(
            jax.ShapeDtypeStruct((CORES, per_core * channels, LAGS), f32),
            jax.ShapeDtypeStruct((slot_count, LAGS), f32),
        ),
        in_specs=[hbm, hbm, hbm, hbm, hbm],
        out_specs=(hbm, hbm),
        scratch_shapes=[
            pltpu.VMEM(das_records.shape, f32),
            pltpu.VMEM(tables.shape, jnp.bfloat16),
            pltpu.VMEM((2 * NEAR * WIN, LPAD), f32),
            pltpu.VMEM((channels + 2 * NEAR, WIN, 2 * NB), f32),
            pltpu.VMEM((WIN, channels, 2 * NB), f32),
            pltpu.VMEM((SOURCES, WIN) + tile, f32),
            pltpu.VMEM((per_core, WIN) + tile, f32),
            pltpu.VMEM((per_core, WIN) + tile, f32),
            pltpu.VMEM((ys - 1,) + block, f32),
            pltpu.VMEM((zs - 1,) + block, f32),
            pltpu.VMEM((zs - 1,) + block, f32),
            pltpu.VMEM((ys - 1,) + block, f32),
            pltpu.VMEM((4,) + block, f32),
            pltpu.VMEM((2, xs, 2) + block, f32),
            pltpu.VMEM((CORES, 2, group, WIN) + tile, f32),
            pltpu.VMEM((SOURCES, channels, 2 * NB), f32),
            pltpu.VMEM((slot_count, 2 * NB), f32),
            pltpu.VMEM((CORES, per_core * channels, LAGS), f32),
            pltpu.VMEM((slot_count, LAGS), f32),
            pltpu.SMEM(source_ids.shape[::-1], jnp.int32),
            pltpu.SMEM(near_pairs.shape[::-1], jnp.int32),
            pltpu.SMEM(pair_count.shape, jnp.int32),
            pltpu.SemaphoreType.DMA((7 + WIN,)),
            pltpu.SemaphoreType.DMA((n_copies,)),
            pltpu.SemaphoreType.DMA((n_copies,)),
        ],
        compiler_params=pltpu.CompilerParams(
            collective_id=0, has_side_effects=True, vmem_limit_bytes=VMEM_LIMIT),
        name="correlate_all",
    )(source_ids.T, near_pairs.T, pair_count, das_records, jnp.asarray(tables))
    source_xcorr, pair_xcorr = pl.pallas_call(
        deliver,
        out_shape=(
            jax.ShapeDtypeStruct(source_xcorr.shape, f32),
            jax.ShapeDtypeStruct(pair_xcorr.shape, f32),
        ),
        in_specs=[hbm, hbm],
        out_specs=(hbm, hbm),
        scratch_shapes=[
            pltpu.VMEM(source_xcorr.shape, f32),
            pltpu.VMEM(pair_xcorr.shape, f32),
            pltpu.SemaphoreType.DMA((2, 2 * PARTS)),
        ],
        compiler_params=pltpu.CompilerParams(vmem_limit_bytes=VMEM_LIMIT),
        name="deliver",
    )(source_xcorr, pair_xcorr)
    return source_xcorr.reshape(source_ids.shape + (channels, LAGS)), pair_xcorr


def solution(mesh, xs=X_CHIPS):
    dims = (xs, mesh.shape["chan"] // xs, mesh.shape["seg"] // CORES)
    in_specs = (P(("seg", "chan"), None, None), P(), P(("seg", "chan"), None), P(("seg", "chan")))
    out_specs = (P(None, None, ("seg", "chan"), None), P(("seg", "chan"), None))
    return jax.shard_map(
        functools.partial(shards, dims), mesh=mesh, in_specs=in_specs, out_specs=out_specs, check_vma=False
    )
```

```python
import functools
import math

import jax
import jax.numpy as jnp
import ml_dtypes
import numpy as np
from jax import lax
from jax.experimental import pallas as pl
from jax.experimental.pallas import tpu as pltpu
from jax.sharding import PartitionSpec as P

WIN = 8
L = 1500
HALF = L // 2
LPAD = 1536
KPAD = 768
FLO = 30
NB = 512
EVEN = NB // 2
SMOOTH = 4
LAGS = 256
SOURCES = 8
NEAR = 8
ROWS = 8
LANES = 128
CORES = 2
X_CHIPS = 4
PARTS = 2

clip_level = 2.0
water_level = 0.1
epsilon = 1e-06

SMOOTH_AT = 4 * KPAD
LAG_AT = SMOOTH_AT + NB
TABLE_ROWS = LAG_AT + 2 * NB

MESH = pl.DeviceIdType.MESH
VMEM_LIMIT = 62 * 1024 * 1024


def split(table):
    high = table.astype(np.float32).astype(ml_dtypes.bfloat16)
    low = (table - high.astype(np.float64)).astype(np.float32).astype(ml_dtypes.bfloat16)
    return high, low


def bin_order():
    return np.concatenate([np.arange(0, NB, 2), np.arange(1, NB, 2)])


@functools.lru_cache(maxsize=None)
def band_tables():
    sample = np.arange(HALF)
    out = np.zeros((2, 2, KPAD, NB), ml_dtypes.bfloat16)
    for parity in range(2):
        freq = FLO + np.arange(parity, NB, 2)
        phase = (sample[:, None] * freq[None, :] % L) * (2.0 * math.pi / L)
        table = np.concatenate([np.cos(phase), -np.sin(phase)], axis=1)
        out[parity, 0, :HALF], out[parity, 1, :HALF] = split(table)
    return out


@functools.lru_cache(maxsize=None)
def lag_tables():
    freq = FLO + bin_order()
    lag = np.arange(LAGS) - LAGS // 2
    phase = (freq[:, None] * lag[None, :] % L) * (2.0 * math.pi / L)
    table = np.concatenate([np.cos(phase), -np.sin(phase)], axis=0) / math.sqrt(WIN * NB)
    return np.stack(split(table))


@functools.lru_cache(maxsize=None)
def smooth_table():
    count = np.zeros((NB, NB))
    for centre in range(NB):
        for step in range(-SMOOTH, SMOOTH + 1):
            count[min(max(centre + step, 0), NB - 1), centre] += 1
    order = bin_order()
    return count[order][:, order].astype(ml_dtypes.bfloat16)


def all_tables():
    band = band_tables().reshape(SMOOTH_AT, NB)
    lags = np.concatenate(list(lag_tables()), axis=1)
    return np.concatenate([band, smooth_table(), lags], axis=0)


def dot(a, b):
    return jnp.dot(a, b, preferred_element_type=jnp.float32)


def halves(value):
    high = value.astype(jnp.bfloat16)
    return high, (value - high.astype(jnp.float32)).astype(jnp.bfloat16)


def dot3(value, high_table, low_table):
    high, low = halves(value)
    rows = value.shape[0]
    both = dot(jnp.concatenate([high, low], axis=0), high_table)
    return both[:rows] + both[rows:] + dot(high, low_table)


def normalize_into(records, padded):
    centered = records - jnp.sum(records, axis=-1, keepdims=True) * (1.0 / L)
    power = jnp.sum(centered * centered, axis=-1, keepdims=True) * (1.0 / L)
    normed = jnp.clip(centered * (1.0 / jnp.sqrt(power + epsilon)), -clip_level, clip_level)
    padded[:, :L] = normed


def spectra_of(padded, tables):
    first = padded[:, :KPAD]
    second = pltpu.roll(padded[...], LPAD - HALF, 1)[:, :KPAD]
    even = dot3(first + second, tables[:KPAD], tables[KPAD : 2 * KPAD])
    odd = dot3(first - second, tables[2 * KPAD : 3 * KPAD], tables[3 * KPAD : SMOOTH_AT])
    real = jnp.concatenate([even[:, :EVEN], odd[:, :EVEN]], axis=1)
    imag = jnp.concatenate([even[:, EVEN:], odd[:, EVEN:]], axis=1)
    amplitude = jnp.sqrt(real * real + imag * imag)
    high, low = halves(amplitude)
    smooth = tables[SMOOTH_AT:LAG_AT]
    rows = amplitude.shape[0]
    both = dot(jnp.concatenate([high, low], axis=0), smooth)
    smoothed = (both[:rows] + both[rows:]) * (1.0 / (2 * SMOOTH + 1))
    mean = jnp.sum(amplitude, axis=-1, keepdims=True) * (water_level / NB)
    scale = 1.0 / (smoothed + mean + epsilon)
    return real * scale, imag * scale


def far_first(n):
    return sorted(range(1, n), key=lambda d: -min(d, n - d))


def kernel(dims, ids_hbm, pairs_hbm, count_hbm, records_hbm, tables_hbm, source_out, pair_out,
           records, tables, padded, near, by_window, kept, half, r0, ra1, rb1, ra2, rb2,
           piece, r3, sources, acc, pair_cross, source_res, pair_res, ids, pairs, count, load, send, recv):
    xs, ys, zs = dims
    seg, chan = lax.axis_index("seg"), lax.axis_index("chan")
    n_chan = lax.axis_size("chan")
    total = lax.axis_size("seg") * n_chan
    me = seg * n_chan + chan
    z, core = seg // CORES, lax.rem(seg, CORES)
    y, x = chan // xs, lax.rem(chan, xs)
    channels = records.shape[0]
    base = me * channels
    per_core = SOURCES // CORES
    group = per_core // 2
    span = WIN // ys

    def at(z_, core_, y_, x_):
        return (z_ * CORES + core_, y_ * xs + x_)

    def of(index):
        return (index // n_chan, lax.rem(index, n_chan))

    def at_x(d):
        return at(z, core, y, lax.rem(x + d, xs))

    def at_x_other(d):
        return at(z, 1 - core, y, lax.rem(x + d, xs))

    def at_y(d):
        return at(z, core, lax.rem(y + d, ys), x)

    def at_z(d):
        return at(lax.rem(z + d, zs), core, y, x)

    sibling = at(z, 1 - core, y, x)
    after = of(lax.rem(me + 1, total))
    before = of(lax.rem(me + total - 1, total))

    barrier = pltpu.get_barrier_semaphore()
    y_far, x_far = far_first(ys), far_first(xs)
    greeted = [there(d) for d in y_far for there in (at_y, at_z)]
    greeted += [there(d) for d in x_far for there in (at_x, at_x_other)] + [after, before, sibling]
    for device in greeted:
        pl.semaphore_signal(barrier, inc=1, device_id=device, device_id_type=MESH)

    numbers = [
        pltpu.make_async_copy(src, dst, load.at[4 + k])
        for k, (src, dst) in enumerate([(ids_hbm, ids), (pairs_hbm, pairs), (count_hbm, count)])
    ]
    numbers[0].start()
    loads = [pltpu.make_async_copy(records_hbm, records, load.at[0])] + [
        pltpu.make_async_copy(tables_hbm.at[lo:hi], tables.at[lo:hi], load.at[1 + k])
        for k, (lo, hi) in enumerate([(0, SMOOTH_AT), (SMOOTH_AT, LAG_AT), (LAG_AT, TABLE_ROWS)])
    ]
    for c in loads[:3] + numbers[1:]:
        c.start()

    tail = padded.shape[0]
    padded[:, LPAD - LANES :] = jnp.zeros((tail, LANES), jnp.float32)

    numbers[0].wait()
    loads[0].wait()
    rows = [records[jnp.clip(ids[s % 2, s // 2] - base, 0, channels - 1)] for s in range(SOURCES)]
    block = jnp.concatenate(rows, axis=0)
    owned = padded.at[pl.ds(0, SOURCES * WIN)]
    normalize_into(block, owned)
    loads[1].wait()
    loads[2].wait()
    real, imag = spectra_of(owned, tables)
    for s in range(SOURCES):
        local = ids[s % 2, s // 2] - base
        mine = jnp.logical_and(local >= 0, local < channels).astype(jnp.float32)
        for r in range(ROWS):
            part = real if r < ROWS // 2 else imag
            lane = (r % (ROWS // 2)) * LANES
            kept[s, :, r, :] = part[s * WIN : (s + 1) * WIN, lane : lane + LANES] * mine

    used = [0]

    def slots(number):
        first = used[0]
        used[0] += number
        return first

    def remote(k, src, dst, device):
        return pltpu.make_async_remote_copy(
            src_ref=src, dst_ref=dst, send_sem=send.at[k], recv_sem=recv.at[k],
            device_id=device, device_id_type=MESH)

    def start(copies):
        for c in copies:
            c.start()
        return copies

    def arrive(copies):
        for c in copies:
            c.wait_recv()

    def spectra_to_near(places):
        block = jnp.concatenate([records[lo:hi] for lo, hi in places], axis=0)
        normalize_into(block.reshape(-1, L), padded)
        real, imag = spectra_of(padded, tables)
        row = 0
        for lo, hi in places:
            size = hi - lo
            near[NEAR + lo : NEAR + hi, :, :NB] = real[row * WIN : (row + size) * WIN].reshape(size, WIN, NB)
            near[NEAR + lo : NEAR + hi, :, NB:] = imag[row * WIN : (row + size) * WIN].reshape(size, WIN, NB)
            row += size

    pl.semaphore_wait(barrier, len(greeted))
    k = slots(1)
    core_copy = start([remote(k, kept.at[pl.ds(per_core * (1 - core), per_core)], r0, sibling)])
    arrive(core_copy)
    half[...] = kept[pl.ds(per_core * core, per_core)] + r0[...]

    def to(d, mine, n):
        return pl.ds(lax.rem(mine + d, n) * span, span)

    ka, kb = slots(ys), slots(zs)
    first = start(
        [c for d in y_far for c in (
            remote(ka + d, half.at[pl.ds(0, group), to(d, y, ys)], ra1.at[d - 1], at_y(d)),
            remote(kb + d, half.at[pl.ds(group, group), to(d, z, zs)], rb1.at[d - 1], at_z(d)))])
    loads[3].start()
    acc[...] = jnp.zeros_like(acc)

    spectra_to_near([(0, NEAR), (channels - NEAR, channels)])
    k_halo = slots(4)

    def halo_part(p):
        size = NEAR // 2
        up, down = channels + p * size, NEAR + p * size
        return start([
            remote(k_halo + 2 * p, near.at[pl.ds(up, size)], near.at[pl.ds(up - channels, size)], after),
            remote(k_halo + 2 * p + 1, near.at[pl.ds(down, size)], near.at[pl.ds(down + channels, size)], before)])

    halo = halo_part(0)
    spectra_to_near([(NEAR, channels - NEAR)])
    turned = [
        pltpu.make_async_copy(near.at[pl.ds(NEAR, channels), w], by_window.at[w], load.at[7 + w])
        for w in range(WIN)
    ]
    for c in turned:
        c.start()

    arrive(first)
    piece[0] = half[:group, pl.ds(y * span, span)] + sum(ra1[d] for d in range(ys - 1))
    piece[1] = half[group:, pl.ds(z * span, span)] + sum(rb1[d] for d in range(zs - 1))
    ka, kb = slots(zs), slots(ys)
    second = start(
        [c for d in y_far for c in (
            remote(ka + d, piece.at[0], ra2.at[d - 1], at_z(d)),
            remote(kb + d, piece.at[1], rb2.at[d - 1], at_y(d)))])
    halo += halo_part(1)
    arrive(second)
    piece[2] = piece[0] + sum(ra2[d] for d in range(zs - 1))
    piece[3] = piece[1] + sum(rb2[d] for d in range(ys - 1))
    k = slots(2 * xs)
    summed = piece.at[pl.ds(2, 2)]
    third = start(
        [c for d in x_far for c in (
            remote(k + xs + d, summed, r3.at[1, d], at_x_other(d)), remote(k + d, summed, r3.at[0, d], at_x(d)))]
        + [remote(k + xs, summed, r3.at[1, 0], sibling)])

    arrive(halo)
    numbers[1].wait()
    slot_count = pair_cross.shape[0]

    def one_pair(slot, carry):
        left = near[jnp.clip(pairs[0, slot] - base + NEAR, 0, channels + 2 * NEAR - 1)]
        right = near[jnp.clip(pairs[1, slot] - base + NEAR, 0, channels + 2 * NEAR - 1)]
        l_re, l_im, r_re, r_im = left[:, :NB], left[:, NB:], right[:, :NB], right[:, NB:]
        pair_cross[pl.ds(slot, 1), :NB] = jnp.sum(l_re * r_re + l_im * r_im, axis=0, keepdims=True)
        pair_cross[pl.ds(slot, 1), NB:] = jnp.sum(l_re * r_im - l_im * r_re, axis=0, keepdims=True)
        return carry

    lax.fori_loop(0, slot_count, one_pair, 0, unroll=4)

    arrive(third)
    for c, whole in ((core, piece[2:] + sum(r3[0, d] for d in range(1, xs))), (1 - core, sum(r3[1, d] for d in range(xs)))):
        sources[c, 0, :, pl.ds(y * span, span)] = whole[0]
        sources[c, 1, :, pl.ds(z * span, span)] = whole[1]
    ka, kb = slots(ys), slots(zs)

    def gather_a(d):
        block = sources.at[:, 0, :, pl.ds(y * span, span)]
        return remote(ka + d, block, block, at_y(d))

    def gather_b(d):
        block = sources.at[:, 1, :, pl.ds(z * span, span)]
        return remote(kb + d, block, block, at_z(d))

    fourth = start([g(d) for d in y_far for g in (gather_a, gather_b)])

    for c in loads[3:] + turned:
        c.wait()
    numbers[2].wait()
    result = dot3(pair_cross[...], tables[LAG_AT:, :LAGS], tables[LAG_AT:, LAGS:])
    live = lax.broadcasted_iota(jnp.int32, (slot_count, 1), 0) < count[0]
    pair_res[...] = result * live.astype(jnp.float32)
    pair_store = pltpu.make_async_copy(pair_res, pair_out, load.at[0])
    pair_store.start()

    def add_blocks(*distances):
        for h, (mine, n) in enumerate(((y, ys), (z, zs))):
            windows = [lax.rem(mine + n - d, n) * span + v for d in distances for v in range(span)]
            for t in range(ROWS // 2):
                re, im = slice(t * LANES, (t + 1) * LANES), slice(NB + t * LANES, NB + (t + 1) * LANES)
                local = [(by_window[w, :, re], by_window[w, :, im]) for w in windows]
                for c in range(CORES):
                    for g in range(group):
                        s = (c * 2 + h) * group + g
                        sum_re, sum_im = acc[s, :, re], acc[s, :, im]
                        for w, (c_re, c_im) in zip(windows, local):
                            s_re = sources[c, h, g, w, t : t + 1]
                            s_im = sources[c, h, g, w, ROWS // 2 + t : ROWS // 2 + t + 1]
                            sum_re += s_re * c_re + s_im * c_im
                            sum_im += s_re * c_im - s_im * c_re
                        acc[s, :, re] = sum_re
                        acc[s, :, im] = sum_im

    add_blocks(0)

    def step(i, carry):
        for d in (i, ys - i):
            gather_a(d).wait_recv()
            gather_b(d).wait_recv()
        add_blocks(i, ys - i)
        return carry

    lax.fori_loop(1, ys // 2, step, 0)
    gather_a(ys // 2).wait_recv()
    gather_b(ys // 2).wait_recv()
    add_blocks(ys // 2)
    lagged = dot3(acc[...].reshape(SOURCES * channels, 2 * NB), tables[LAG_AT:, :LAGS], tables[LAG_AT:, LAGS:])
    stores = []
    for c in range(CORES):
        source_res[c] = lagged[c * per_core * channels : (c + 1) * per_core * channels]
        stores.append(pltpu.make_async_copy(source_res.at[c], source_out.at[c], load.at[1 + c]))
        stores[c].start()
    for c in core_copy + first + halo + second + third + fourth:
        c.wait_send()
    pair_store.wait()
    for c in stores:
        c.wait()


def deliver(source_in, pair_in, source_out, pair_out, source_held, pair_held, sems):
    inward, outward = [], []
    for src, held, dst in ((source_in, source_held, source_out), (pair_in, pair_held, pair_out)):
        rows = src.shape[0] // PARTS
        for p in range(PARTS):
            part = pl.ds(p * rows, rows)
            k = len(inward)
            inward.append(pltpu.make_async_copy(src.at[part], held.at[part], sems.at[0, k]))
            outward.append(pltpu.make_async_copy(held.at[part], dst.at[part], sems.at[1, k]))
    for c in inward:
        c.start()
    for c, o in zip(inward, outward):
        c.wait()
        o.start()
    for o in outward:
        o.wait()


def shards(dims, das_records, source_ids, near_pairs, pair_count):
    xs, ys, zs = dims
    channels = das_records.shape[0]
    slot_count = near_pairs.shape[0]
    hbm = pl.BlockSpec(memory_space=pl.ANY)
    f32 = jnp.float32
    per_core = SOURCES // CORES
    group = per_core // 2
    span = WIN // ys
    tables = all_tables()
    tile = (ROWS, LANES)
    block = (group, span) + tile
    n_copies = 5 + 3 * ys + 3 * zs + 2 * xs
    source_xcorr, pair_xcorr = pl.pallas_call(
        functools.partial(kernel, dims),
        out_shape=(
            jax.ShapeDtypeStruct((CORES, per_core * channels, LAGS), f32),
            jax.ShapeDtypeStruct((slot_count, LAGS), f32),
        ),
        in_specs=[hbm, hbm, hbm, hbm, hbm],
        out_specs=(hbm, hbm),
        scratch_shapes=[
            pltpu.VMEM(das_records.shape, f32),
            pltpu.VMEM(tables.shape, jnp.bfloat16),
            pltpu.VMEM((2 * NEAR * WIN, LPAD), f32),
            pltpu.VMEM((channels + 2 * NEAR, WIN, 2 * NB), f32),
            pltpu.VMEM((WIN, channels, 2 * NB), f32),
            pltpu.VMEM((SOURCES, WIN) + tile, f32),
            pltpu.VMEM((per_core, WIN) + tile, f32),
            pltpu.VMEM((per_core, WIN) + tile, f32),
            pltpu.VMEM((ys - 1,) + block, f32),
            pltpu.VMEM((zs - 1,) + block, f32),
            pltpu.VMEM((zs - 1,) + block, f32),
            pltpu.VMEM((ys - 1,) + block, f32),
            pltpu.VMEM((4,) + block, f32),
            pltpu.VMEM((2, xs, 2) + block, f32),
            pltpu.VMEM((CORES, 2, group, WIN) + tile, f32),
            pltpu.VMEM((SOURCES, channels, 2 * NB), f32),
            pltpu.VMEM((slot_count, 2 * NB), f32),
            pltpu.VMEM((CORES, per_core * channels, LAGS), f32),
            pltpu.VMEM((slot_count, LAGS), f32),
            pltpu.SMEM(source_ids.shape[::-1], jnp.int32),
            pltpu.SMEM(near_pairs.shape[::-1], jnp.int32),
            pltpu.SMEM(pair_count.shape, jnp.int32),
            pltpu.SemaphoreType.DMA((7 + WIN,)),
            pltpu.SemaphoreType.DMA((n_copies,)),
            pltpu.SemaphoreType.DMA((n_copies,)),
        ],
        compiler_params=pltpu.CompilerParams(
            collective_id=0, has_side_effects=True, vmem_limit_bytes=VMEM_LIMIT),
        name="correlate_all",
    )(source_ids.T, near_pairs.T, pair_count, das_records, jnp.asarray(tables))
    source_xcorr, pair_xcorr = pl.pallas_call(
        deliver,
        out_shape=(
            jax.ShapeDtypeStruct(source_xcorr.shape, f32),
            jax.ShapeDtypeStruct(pair_xcorr.shape, f32),
        ),
        in_specs=[hbm, hbm],
        out_specs=(hbm, hbm),
        scratch_shapes=[
            pltpu.VMEM(source_xcorr.shape, f32),
            pltpu.VMEM(pair_xcorr.shape, f32),
            pltpu.SemaphoreType.DMA((2, 2 * PARTS)),
        ],
        compiler_params=pltpu.CompilerParams(vmem_limit_bytes=VMEM_LIMIT),
        name="deliver",
    )(source_xcorr, pair_xcorr)
    return source_xcorr.reshape(source_ids.shape + (channels, LAGS)), pair_xcorr


def solution(mesh, xs=X_CHIPS):
    dims = (xs, mesh.shape["chan"] // xs, mesh.shape["seg"] // CORES)
    in_specs = (P(("seg", "chan"), None, None), P(), P(("seg", "chan"), None), P(("seg", "chan")))
    out_specs = (P(None, None, ("seg", "chan"), None), P(("seg", "chan"), None))
    return jax.shard_map(
        functools.partial(shards, dims), mesh=mesh, in_specs=in_specs, out_specs=out_specs, check_vma=False
    )
```
